32 devices in a mesh: orb: 8 (over z, core), dom: 4 (over y, x).
Axes of the slice: x: 2, y: 2, z: 4, core: 2. Of those that a mesh axis runs over, the one named last changes fastest.
Arguments:
- orbitals: bfloat16 [8, 16, 48, 128], P('orb', None, 'dom'), may hold values from -6 to 6
- potential: float32 [16, 48, 128], P(None, 'dom'), may hold values from 0 to 2
- degree: int32 [8], P('orb'), may hold values from 1 to 8, as said below
- owners: int32 [4], replicated, may hold values from 0 to 7
- rotation: bfloat16 [4, 1, 8], P(None, None, 'orb'), may hold values from -3 to 3
Outputs:
- filtered: float32 [8, 16, 48, 128], P('orb', None, 'dom')
- rotated: float32 [8, 16, 48, 128], P('orb', None, 'dom')
The draws below stay inside these ranges and needn't reach their ends.
Inputs may be any that keep to these rules, and one draw needn't show every extreme that they name: Every draw has an orbital of degree 8 and one of degree 1. `owners`: panel numbers; panel q holds orbital q alone.
All inputs are finite; a program needn't handle non-finite values.
Results may differ from the reference program's by a relative error of at most 0.0003.
Values sent between devices are 32-bit elements; how exact they have to be, the bound alone decides.
No kernel may reach another device: no remote copies, remote signals or barrier semaphores. Data moves between devices by JAX's collectives and lax.ppermute only.
A program may use at most 64 MiB of HBM per device.

```python
import jax
import jax.numpy as jnp
from jax import lax

ORB_DEV = 1
PL = 16
GY = 128
RADIUS = 6
MAXDEG = 8
STEPS = 4
NORB = 8
PANEL = 1
NPANEL = 8
GX = 48
N_ORB = 8


def draw_degree(key, part):
    first_key, second_key, third_key = jax.random.split(key, 3)
    values = jax.random.randint(first_key, (NORB,), 1, MAXDEG + 1)
    top_place = jax.random.randint(second_key, (), 0, NORB)
    low_place = (top_place + 1 + jax.random.randint(third_key, (), 0, NORB - 1)) % NORB
    values = values.at[top_place].set(MAXDEG)
    values = values.at[low_place].set(1)
    return values.astype(jnp.int32)


def plant(drawn, rng, smallest, largest):
    dims = drawn.shape
    place = [jax.random.randint(jax.random.fold_in(rng, axis), (), 0, dims[axis]) for axis in range(len(dims))]
    drawn = drawn.at[tuple(place)].set(smallest)
    longest = dims.index(max(dims))
    place[longest] = (place[longest] + 1) % dims[longest]
    return drawn.at[tuple(place)].set(largest)


def steps_of(stream_key, shape, cuts, least, top_value):
    level = 1.0
    for dim, parts in cuts:
        steps = jax.random.uniform(jax.random.fold_in(jax.random.fold_in(stream_key, 6), dim), (parts,), jnp.float32, least / len(cuts), top_value / len(cuts))
        level = level * jnp.repeat(jnp.exp(steps), shape[dim] // parts).reshape((-1,) + (1,) * (len(shape) - 1 - dim))
    return level


def bell_draw(key, extent, spread, most, pieces=(), kind=jnp.bfloat16):
    factor_of = steps_of(key, extent, pieces, -0.22, 0.18) if pieces else 1.0
    entries = jax.random.normal(key, extent, jnp.float32) * spread * factor_of
    return jnp.minimum(jnp.maximum(entries, -most), most).astype(kind)


def setup_inputs(seed: int = 0) -> dict:
    key_of = jax.random.split(jax.random.key(seed), 6)
    orbitals = bell_draw(key_of[0], (NORB, PL, GX, GY), 1.0, 6.0, ((0, 8), (2, 4)))
    potential = jnp.clip(2.0 * jax.random.uniform(key_of[1], (PL, GX, GY), jnp.float32) ** steps_of(key_of[1], (PL, GX, GY), ((1, 4),), -0.2, 0.2), 0.0, 2.0)
    degree = draw_degree(jax.random.fold_in(key_of[5], 71), 0)
    owners = plant(jax.random.randint(key_of[3], (STEPS,), 0, NPANEL), jax.random.fold_in(key_of[3], 1), 0, NPANEL - 1).astype(jnp.int32)
    rotation = bell_draw(key_of[4], (STEPS, PANEL, NORB), (STEPS * PANEL) ** -0.5, 3.0, ((2, 8),))
    return dict(orbitals=orbitals, potential=potential, degree=degree, owners=owners, rotation=rotation)


STENCIL = (-5369.0 / 1800.0, 12.0 / 7.0, -15.0 / 56.0, 10.0 / 189.0, -1.0 / 112.0, 2.0 / 1925.0, -1.0 / 16632.0)
FILTER_CENTER = 7.75
FILTER_HALF = 6.25


def apply_hamiltonian(padded, potential):
    width = padded.shape[2] - 2 * RADIUS
    center = padded[:, :, RADIUS:RADIUS + width]
    laplace = (3.0 * STENCIL[0]) * center
    for offset in range(1, RADIUS + 1):
        beside = padded[:, :, RADIUS + offset:RADIUS + offset + width] + padded[:, :, RADIUS - offset:RADIUS - offset + width]
        beside = beside + jnp.roll(center, offset, 3) + jnp.roll(center, -offset, 3)
        beside = beside + jnp.roll(center, offset, 1) + jnp.roll(center, -offset, 1)
        laplace = laplace + STENCIL[offset] * beside
    return -0.5 * laplace + potential * center


def chebyshev_next(applied, current, previous, first):
    shifted = applied - FILTER_CENTER * current
    if first:
        return shifted / FILTER_HALF
    return (2.0 / FILTER_HALF) * shifted - previous


def reference(orbitals, potential, degree, owners, rotation):
    blocks = orbitals.reshape(N_ORB, ORB_DEV, PL, GX, GY)
    degrees = degree.reshape(N_ORB, ORB_DEV)

    def one_block(pair):
        block, degree_block = pair
        current = block.astype(jnp.float32)
        previous = current
        selected = jnp.zeros_like(current)
        for section in range(MAXDEG):
            padded = jnp.pad(current, ((0, 0), (0, 0), (RADIUS, RADIUS), (0, 0)))
            applied = apply_hamiltonian(padded, potential)
            advanced = chebyshev_next(applied, current, previous, section == 0)
            selected = jnp.where((degree_block == section + 1)[:, None, None, None], advanced, selected)
            previous, current = current, advanced
        return selected

    filtered = lax.map(one_block, (blocks, degrees)).reshape(NORB, PL, GX, GY)
    flattened = filtered.reshape(NORB, PL * GX * GY)
    rotated = jnp.zeros((NORB, PL * GX * GY), jnp.float32)
    for section in range(STEPS):
        start_row = (owners[section] * PANEL).astype(jnp.int32)
        panel = lax.dynamic_slice_in_dim(flattened, start_row, PANEL, 0)
        coefficients = rotation[section].astype(jnp.float32)
        rotated = rotated + lax.dot_general(coefficients, panel, (((0,), (0,)), ((), ())), precision=lax.Precision.HIGHEST, preferred_element_type=jnp.float32)
    rotated = rotated.reshape(NORB, PL, GX, GY)
    return filtered, rotated
```

```python
import functools

import jax
import jax.numpy as jnp
from jax import lax
from jax.experimental import pallas as pl
from jax.experimental.pallas import tpu as pltpu
from jax.sharding import PartitionSpec as P

RADIUS = 6
MAXDEG = 8
STEPS = 4

STENCIL = (
    -5369.0 / 1800.0,
    12.0 / 7.0,
    -15.0 / 56.0,
    10.0 / 189.0,
    -1.0 / 112.0,
    2.0 / 1925.0,
    -1.0 / 16632.0,
)
FILTER_CENTER = 7.75
FILTER_HALF = 6.25
SCALE = 2.0 / FILTER_HALF
TAPS = tuple(-0.5 * SCALE * c for c in STENCIL[1:])
DIAGONAL = SCALE * (-1.5 * STENCIL[0] - FILTER_CENTER)


def xor_pairs(count, mask):
    return [(i, i ^ mask) for i in range(count)]


def shift_pairs(count, step):
    return [(i, i - step) for i in range(count) if 0 <= i - step < count]


def pack_kernel(orbital_ref, potential_ref, out_ref):
    cells = out_ref.shape[0] // 2
    for x in range(cells):
        out_ref[x] = orbital_ref[0, :, x, :].astype(jnp.float32)
        out_ref[cells + x] = potential_ref[:, x, :]


def chain_kernel(whole, slots, place_ref, *refs):
    blocks = refs[: len(slots)]
    out_ref, sent_ref, even, odd, field = refs[len(slots) :]
    cells = blocks[0].shape[0] // 2
    window = even.shape[0] - 2 * RADIUS
    degree = place_ref[0]
    first = place_ref[1]
    grid_low = place_ref[2]
    grid_high = place_ref[3]

    edge = jnp.zeros((RADIUS,) + even.shape[1:], jnp.float32)
    for ref in (even, odd):
        ref[pl.ds(0, RADIUS)] = edge
        ref[pl.ds(RADIUS + window, RADIUS)] = edge
    if not whole:
        odd[...] = jnp.zeros(odd.shape, jnp.float32)
    for index, block in enumerate(blocks):
        start = place_ref[4 + index]
        even[pl.ds(RADIUS + start, cells)] = block[:cells]
        field[pl.ds(start, cells)] = SCALE * block[cells:] + DIAGONAL

    def step(level, source, target):
        reach = RADIUS * (degree - level)
        low = jnp.maximum(first - reach, grid_low)
        high = jnp.minimum(first + cells + reach, grid_high)

        def body(index, carry):
            base = low + index * RADIUS
            for row in range(RADIUS):
                x = base + row
                center = source[RADIUS + x]
                total = field[x] * center
                for k in range(1, RADIUS + 1):
                    beside = source[RADIUS + x + k] + source[RADIUS + x - k]
                    beside = beside + (pltpu.roll(center, k, 1) + pltpu.roll(center, center.shape[1] - k, 1))
                    beside = beside + (pltpu.roll(center, k, 0) + pltpu.roll(center, center.shape[0] - k, 0))
                    total = total + TAPS[k - 1] * beside
                if level == 1:
                    target[RADIUS + x] = 0.5 * total
                else:
                    target[RADIUS + x] = total - target[RADIUS + x]
            return carry

        lax.fori_loop(0, (high - low) // RADIUS, body, 0)

    for level in range(1, MAXDEG + 1):
        source, target = (even, odd) if level % 2 else (odd, even)
        pl.when(level <= degree)(functools.partial(step, level, source, target))

    def finish(ref):
        for x in range(cells):
            value = ref[RADIUS + first + x]
            sent_ref[x] = value
            out_ref[0, :, x, :] = value

    pl.when(degree % 2 == 0)(functools.partial(finish, even))
    pl.when(degree % 2 == 1)(functools.partial(finish, odd))


def combine_kernel(count, weights_ref, *refs):
    panels, (mine_ref, theirs_ref) = refs[:count], refs[count:]
    for out, ref in enumerate((mine_ref, theirs_ref)):
        total = weights_ref[out, 0] * panels[0][...]
        for index in range(1, count):
            total = total + weights_ref[out, index] * panels[index][...]
        ref[...] = total


def finish_kernel(mine_ref, theirs_ref, out_ref):
    for x in range(mine_ref.shape[0]):
        out_ref[0, :, x, :] = mine_ref[x] + theirs_ref[x]


def per_device(orbitals, potential, degree, owners, rotation):
    _, planes, cells, width = orbitals.shape
    n_dom = lax.axis_size("dom")
    n_orb = lax.axis_size("orb")
    me = lax.axis_index("orb")
    dom = lax.axis_index("dom")
    vmem = pl.BlockSpec(memory_space=pltpu.VMEM)
    smem = pl.BlockSpec(memory_space=pltpu.SMEM)
    f32 = jnp.float32
    slab = (cells, planes, width)
    out_type = jax.ShapeDtypeStruct(orbitals.shape, f32)

    packed = pl.pallas_call(
        pack_kernel,
        out_shape=jax.ShapeDtypeStruct((2 * cells, planes, width), f32),
        in_specs=[vmem, vmem],
        out_specs=vmem,
    )(orbitals, potential)

    halo = -(-RADIUS * MAXDEG // cells)
    whole = n_dom <= 2 * halo + 1
    if whole:
        slots = list(range(n_dom))
        blocks = [packed] + [lax.ppermute(packed, "dom", xor_pairs(n_dom, k)) for k in slots[1:]]
        starts = [(dom ^ k) * cells for k in slots]
        first, grid_low, grid_high, window = dom * cells, 0, n_dom * cells, n_dom * cells
    else:
        slots = [0] + [s * k for k in range(1, halo + 1) for s in (1, -1)]
        blocks = [packed] + [lax.ppermute(packed, "dom", shift_pairs(n_dom, k)) for k in slots[1:]]
        starts = [(halo + k) * cells for k in slots]
        window = (2 * halo + 1) * cells
        first = halo * cells
        grid_low = jnp.maximum(first - dom * cells, 0)
        grid_high = jnp.minimum(first + (n_dom - dom) * cells, window)
    place = jnp.stack([jnp.asarray(v, jnp.int32) for v in [degree[0], first, grid_low, grid_high] + starts])
    buffer = pltpu.VMEM((window + 2 * RADIUS, planes, width), f32)
    filtered, panel = pl.pallas_call(
        functools.partial(chain_kernel, whole, slots),
        out_shape=(out_type, jax.ShapeDtypeStruct(slab, f32)),
        in_specs=[smem] + [vmem] * len(slots),
        out_specs=(vmem, vmem),
        scratch_shapes=[buffer, buffer, pltpu.VMEM((window, planes, width), f32)],
    )(place, *blocks)

    coefficients = rotation[:, 0, 0].astype(f32)
    beside = lax.ppermute(coefficients, "orb", xor_pairs(n_orb, 1))
    masks = sorted(range(2, n_orb, 2), key=lambda m: -m)
    panels = [panel] + [lax.ppermute(panel, "orb", xor_pairs(n_orb, m)) for m in masks]
    held = jnp.stack([me ^ m for m in [0] + masks])
    chosen = (owners[:, None] == held[None, :]).astype(f32)
    weights = jnp.stack([jnp.sum(c[:, None] * chosen, 0) for c in (coefficients, beside)])
    mine, theirs = pl.pallas_call(
        functools.partial(combine_kernel, len(panels)),
        out_shape=(jax.ShapeDtypeStruct(slab, f32),) * 2,
        in_specs=[smem] + [vmem] * len(panels),
        out_specs=(vmem, vmem),
    )(weights, *panels)
    arrived = lax.ppermute(theirs, "orb", xor_pairs(n_orb, 1))
    rotated = pl.pallas_call(
        finish_kernel,
        out_shape=out_type,
        in_specs=[vmem, vmem],
        out_specs=vmem,
    )(mine, arrived)
    return filtered, rotated


def solution(mesh):
    placed = (
        P("orb", None, "dom", None),
        P(None, "dom", None),
        P("orb"),
        P(),
        P(None, None, "orb"),
    )
    return jax.shard_map(
        per_device,
        mesh=mesh,
        in_specs=placed,
        out_specs=(P("orb", None, "dom", None), P("orb", None, "dom", None)),
        check_vma=False,
    )
```

```python
import functools

import jax
import jax.numpy as jnp
from jax import lax
from jax.experimental import pallas as pl
from jax.experimental.pallas import tpu as pltpu
from jax.sharding import PartitionSpec as P

RADIUS = 6
MAXDEG = 8
STEPS = 4

STENCIL = (
    -5369.0 / 1800.0,
    12.0 / 7.0,
    -15.0 / 56.0,
    10.0 / 189.0,
    -1.0 / 112.0,
    2.0 / 1925.0,
    -1.0 / 16632.0,
)
FILTER_CENTER = 7.75
FILTER_HALF = 6.25
SCALE = 2.0 / FILTER_HALF
TAPS = tuple(-0.5 * SCALE * c for c in STENCIL[1:])
DIAGONAL = SCALE * (-1.5 * STENCIL[0] - FILTER_CENTER)


def xor_pairs(count, mask):
    return [(i, i ^ mask) for i in range(count)]


def shift_pairs(count, step):
    return [(i, i - step) for i in range(count) if 0 <= i - step < count]


def chain_kernel(whole, slots, n_dom, degree_ref, *refs):
    blocks = refs[: len(slots)]
    out_ref, even, odd, field = refs[len(slots) :]
    cells = blocks[0].shape[0] // 2
    window = even.shape[0] - 2 * RADIUS
    degree = degree_ref[0]
    dom = lax.axis_index("dom")
    if whole:
        starts = [(dom ^ k) * cells for k in slots]
        first, grid_low, grid_high = dom * cells, 0, window
    else:
        middle = window // 2 // cells * cells
        starts = [middle + k * cells for k in slots]
        first = middle
        grid_low = jnp.maximum(first - dom * cells, 0)
        grid_high = jnp.minimum(first + (n_dom - dom) * cells, window)

    edge = jnp.zeros((RADIUS,) + even.shape[1:], jnp.float32)
    for ref in (even, odd):
        ref[pl.ds(0, RADIUS)] = edge
        ref[pl.ds(RADIUS + window, RADIUS)] = edge
    if not whole:
        odd[...] = jnp.zeros(odd.shape, jnp.float32)
    for start, block in zip(starts, blocks):
        even[pl.ds(RADIUS + start, cells)] = block[:cells]
        field[pl.ds(start, cells)] = SCALE * block[cells:] + DIAGONAL

    def step(level, source, target):
        reach = RADIUS * (degree - level)
        low = jnp.maximum(first - reach, grid_low)
        high = jnp.minimum(first + cells + reach, grid_high)

        def body(index, carry):
            base = low + index * RADIUS
            for row in range(RADIUS):
                x = base + row
                center = source[RADIUS + x]
                total = field[x] * center
                for k in range(1, RADIUS + 1):
                    beside = source[RADIUS + x + k] + source[RADIUS + x - k]
                    beside = beside + (pltpu.roll(center, k, 1) + pltpu.roll(center, center.shape[1] - k, 1))
                    beside = beside + (pltpu.roll(center, k, 0) + pltpu.roll(center, center.shape[0] - k, 0))
                    total = total + TAPS[k - 1] * beside
                if level == 1:
                    target[RADIUS + x] = 0.5 * total
                else:
                    target[RADIUS + x] = total - target[RADIUS + x]
            return carry

        lax.fori_loop(0, (high - low) // RADIUS, body, 0)

    for level in range(1, MAXDEG + 1):
        source, target = (even, odd) if level % 2 else (odd, even)
        pl.when(level <= degree)(functools.partial(step, level, source, target))

    def finish(ref):
        out_ref[...] = ref[pl.ds(RADIUS + first, cells)]

    pl.when(degree % 2 == 0)(functools.partial(finish, even))
    pl.when(degree % 2 == 1)(functools.partial(finish, odd))


def combine_kernel(masks, owners_ref, mine_ref, theirs_ref, *refs):
    panels, outs = refs[: len(masks)], refs[len(masks) :]
    me = lax.axis_index("orb")
    for out, coefficients in zip(outs, (mine_ref, theirs_ref)):
        total = None
        for mask, panel in zip(masks, panels):
            weight = jnp.float32(0)
            for step in range(STEPS):
                weight = weight + jnp.where(owners_ref[step] == me ^ mask, coefficients[step], 0.0)
            term = weight * panel[...]
            total = term if total is None else total + term
        out[...] = total


def in_vmem(x):
    return pltpu.with_memory_space_constraint(x, pltpu.VMEM)


def per_device(orbitals, potential, degree, owners, rotation):
    _, planes, cells, width = orbitals.shape
    n_dom = lax.axis_size("dom")
    n_orb = lax.axis_size("orb")
    vmem = pl.BlockSpec(memory_space=pltpu.VMEM)
    smem = pl.BlockSpec(memory_space=pltpu.SMEM)
    f32 = jnp.float32
    slab = pltpu.VMEM((cells, planes, width), f32)

    orbital = jnp.transpose(orbitals[0], (1, 0, 2)).astype(f32)
    packed = jnp.concatenate([orbital, jnp.transpose(potential, (1, 0, 2))], 0)

    halo = -(-RADIUS * MAXDEG // cells)
    whole = n_dom <= 2 * halo + 1
    if whole:
        slots = list(range(n_dom))
        blocks = [packed] + [lax.ppermute(packed, "dom", xor_pairs(n_dom, k)) for k in slots[1:]]
        window = n_dom * cells
    else:
        slots = [0] + [s * k for k in range(1, halo + 1) for s in (1, -1)]
        blocks = [packed] + [lax.ppermute(packed, "dom", shift_pairs(n_dom, k)) for k in slots[1:]]
        window = (2 * halo + 1) * cells
    buffer = pltpu.VMEM((window + 2 * RADIUS, planes, width), f32)
    panel = pl.pallas_call(
        functools.partial(chain_kernel, whole, slots, n_dom),
        out_shape=slab,
        in_specs=[smem] + [vmem] * len(slots),
        out_specs=vmem,
        scratch_shapes=[buffer, buffer, pltpu.VMEM((window, planes, width), f32)],
    )(degree, *[in_vmem(b) for b in blocks])

    coefficients = rotation[:, 0, 0].astype(f32)
    beside = lax.ppermute(coefficients, "orb", xor_pairs(n_orb, 1))
    masks = sorted(range(2, n_orb, 2), key=lambda m: -m)
    panels = [panel] + [lax.ppermute(panel, "orb", xor_pairs(n_orb, m)) for m in masks]
    mine, theirs = pl.pallas_call(
        functools.partial(combine_kernel, [0] + masks),
        out_shape=(slab, slab),
        in_specs=[smem] * 3 + [vmem] * len(panels),
        out_specs=(vmem, vmem),
    )(owners, coefficients, beside, *[in_vmem(p) for p in panels])
    rotated = mine + lax.ppermute(theirs, "orb", xor_pairs(n_orb, 1))
    return tuple(jnp.transpose(x, (1, 0, 2))[None] for x in (panel, rotated))


def solution(mesh):
    placed = (
        P("orb", None, "dom", None),
        P(None, "dom", None),
        P("orb"),
        P(),
        P(None, None, "orb"),
    )
    return jax.shard_map(
        per_device,
        mesh=mesh,
        in_specs=placed,
        out_specs=(P("orb", None, "dom", None), P("orb", None, "dom", None)),
        check_vma=False,
    )
```

```python
import functools

import jax
import jax.numpy as jnp
import ml_dtypes
import numpy as np
from jax import lax
from jax.experimental import pallas as pl
from jax.experimental.pallas import tpu as pltpu
from jax.sharding import PartitionSpec as P

RADIUS = 6
MAXDEG = 8
STEPS = 4

STENCIL = (
    -5369.0 / 1800.0,
    12.0 / 7.0,
    -15.0 / 56.0,
    10.0 / 189.0,
    -1.0 / 112.0,
    2.0 / 1925.0,
    -1.0 / 16632.0,
)
FILTER_CENTER = 7.75
FILTER_HALF = 6.25
SCALE = 2.0 / FILTER_HALF
TAPS = tuple(-0.5 * SCALE * c for c in STENCIL[1:])
DIAGONAL = SCALE * (-1.5 * STENCIL[0] - FILTER_CENTER)


def xor_pairs(count, mask):
    return [(i, i ^ mask) for i in range(count)]


def shift_pairs(count, step):
    return [(i, i - step) for i in range(count) if 0 <= i - step < count]


def split(values):
    high = values.astype(jnp.bfloat16)
    return high, (values - high.astype(jnp.float32)).astype(jnp.bfloat16)


def ring(count, copies):
    matrix = np.zeros((count, count), np.float64)
    for k, tap in enumerate(TAPS, 1):
        for i in range(count):
            matrix[i, (i + k) % count] += tap
            matrix[i, (i - k) % count] += tap
    matrix = np.kron(np.eye(copies), matrix)
    high = matrix.astype(ml_dtypes.bfloat16)
    low = (matrix - high.astype(np.float64)).astype(ml_dtypes.bfloat16)
    return high, low


def chain_kernel(whole, slots, groups, n_dom, degree_ref, rows_ref, *refs):
    planes_at = dict(zip(groups, refs))
    refs = refs[len(groups) :]
    blocks = refs[: len(slots)]
    out_ref, *fields, potential = refs[len(slots) :]
    cells = blocks[0].shape[0] // 2
    planes, width = potential.shape[1:]
    window = potential.shape[0]
    n_blocks = window // cells
    degree = degree_ref[0]
    dom = lax.axis_index("dom")
    home = dom if whole else n_blocks // 2
    starts = [(dom ^ k if whole else home + k) * cells for k in slots]
    rows = cells * planes

    for start, block in zip(starts, blocks):
        potential[pl.ds(start, cells)] = SCALE * block[cells:] + DIAGONAL
    for ref in fields:
        ref[pl.ds(0, RADIUS)] = jnp.zeros((RADIUS, planes, width), jnp.float32)
        ref[pl.ds(RADIUS + window, RADIUS)] = jnp.zeros((RADIUS, planes, width), jnp.float32)

    def begin(current, previous):
        for start, block in zip(starts, blocks):
            current[pl.ds(RADIUS + start, cells)] = block[:cells]
        previous[pl.ds(RADIUS, window)] = jnp.zeros((window, planes, width), jnp.float32)

    pl.when(degree % 2 == 0)(functools.partial(begin, fields[0], fields[1]))
    pl.when(degree % 2 == 1)(functools.partial(begin, fields[1], fields[0]))

    def advance(parity, factor, start, count):
        source, target = fields[1 - parity], fields[parity]
        base = start * cells
        high, low = split(source[pl.ds(RADIUS + base, count * cells)].reshape(count * rows, width))
        both = jnp.concatenate([high, low], 1)
        across = jnp.dot(both, rows_ref[...], preferred_element_type=jnp.float32)
        group = max(m for m in planes_at if count * cells % (2 * m) == 0)
        size = group * planes
        alongs = []
        for top in range(0, count * rows, 2 * size):
            pieces = [jnp.concatenate([v[top : top + size], v[top + size : top + 2 * size]], 1) for v in (high, low)]
            alongs.append(
                jnp.dot(
                    planes_at[group][...], jnp.concatenate(pieces, 0), preferred_element_type=jnp.float32
                )
            )
        for part in range(0, count * cells, RADIUS):
            x = base + part
            near = source[pl.ds(x, 3 * RADIUS)]
            total = potential[pl.ds(x, RADIUS)] * near[RADIUS : 2 * RADIUS]
            for k in range(1, RADIUS + 1):
                beside = near[RADIUS + k : 2 * RADIUS + k] + near[RADIUS - k : 2 * RADIUS - k]
                total = total + TAPS[k - 1] * beside
            spot = pl.ds(RADIUS + x, RADIUS)
            target[spot] = factor * total - target[spot]
        for index, along in enumerate(alongs):
            along = along[:size] + along[size:]
            for half in range(2):
                top = (2 * index + half) * size
                plane_sum = across[top : top + size, :width] + across[top : top + size, width:]
                plane_sum = plane_sum + along[:, half * width : (half + 1) * width]
                spot = pl.ds(RADIUS + base + (2 * index + half) * group, group)
                target[spot] = target[spot] + factor * plane_sum.reshape(group, planes, width)

    def level(left, parity, reach):
        count = min(2 * reach + 1, n_blocks)
        factor = jnp.where(left == degree - 1, 0.5, 1.0)
        if whole:
            advance(parity, factor, jnp.clip(home - reach, 0, n_blocks - count), count)
            return
        for block in range(home - reach, home - reach + count):
            place = dom + block - home
            pl.when((place >= 0) & (place < n_dom))(functools.partial(advance, parity, factor, block, 1))

    def levels(fewest, most, reach):
        top = jnp.minimum(most, degree - 1)
        parity = fewest % 2

        def pair(index, carry):
            left = fewest + 2 * (count // 2 - index) - 1
            level(left, 1 - parity, reach)
            level(left - 1, parity, reach)
            return carry

        count = jnp.maximum(top - fewest + 1, 0)
        if most > fewest:
            pl.when(count % 2 == 1)(lambda: level(top, parity, reach))
            lax.fori_loop(0, count // 2, pair, 0)
        else:
            pl.when(count == 1)(lambda: level(fewest, parity, reach))

    bounds = [-(-RADIUS * left // cells) for left in range(MAXDEG)]
    if whole:
        bounds = [min(reach, n_blocks // 2) for reach in bounds]
    for reach in sorted(set(bounds), reverse=True):
        lefts = [left for left in range(MAXDEG) if bounds[left] == reach]
        levels(lefts[0], lefts[-1], reach)
    out_ref[...] = fields[0][pl.ds(RADIUS + home * cells, cells)]


def combine_kernel(masks, owners_ref, mine_ref, theirs_ref, *refs):
    panels, outs = refs[: len(masks)], refs[len(masks) :]
    me = lax.axis_index("orb")
    for out, coefficients in zip(outs, (mine_ref, theirs_ref)):
        total = None
        for mask, panel in zip(masks, panels):
            weight = jnp.float32(0)
            for step in range(STEPS):
                weight = weight + jnp.where(owners_ref[step] == me ^ mask, coefficients[step], 0.0)
            term = weight * panel[...]
            total = term if total is None else total + term
        out[...] = total


def in_vmem(x):
    return pltpu.with_memory_space_constraint(x, pltpu.VMEM)


def chain(degree, blocks, n_dom):
    cells, planes, width = blocks[0].shape[0] // 2, *blocks[0].shape[1:]
    halo = -(-RADIUS * MAXDEG // cells)
    whole = n_dom <= 2 * halo + 1
    if whole:
        slots = list(range(n_dom))
        window = n_dom * cells
        counts = range(1, n_dom + 1)
    else:
        slots = [0] + [s * k for k in range(1, halo + 1) for s in (1, -1)]
        window = (2 * halo + 1) * cells
        counts = [1]
    high, low = ring(width, 1)
    across = np.block([[high, low], [high, low]])
    groups = sorted({max(g for g in range(1, width // planes + 1) if c * cells % (2 * g) == 0) for c in counts})
    alongs = [np.block([[m, m] for m in ring(planes, g)]) for g in groups]
    field = pltpu.VMEM((window + 2 * RADIUS, planes, width), jnp.float32)
    vmem = pl.BlockSpec(memory_space=pltpu.VMEM)
    smem = pl.BlockSpec(memory_space=pltpu.SMEM)
    return pl.pallas_call(
        functools.partial(chain_kernel, whole, slots, groups, n_dom),
        out_shape=pltpu.VMEM((cells, planes, width), jnp.float32),
        in_specs=[smem] + [vmem] * (1 + len(groups) + len(slots)),
        out_specs=vmem,
        scratch_shapes=[field, field, pltpu.VMEM((window, planes, width), jnp.float32)],
    )(degree, *[in_vmem(b) for b in [jnp.asarray(m) for m in [across] + alongs] + blocks])


def per_device(orbitals, potential, degree, owners, rotation):
    _, planes, cells, width = orbitals.shape
    n_dom = lax.axis_size("dom")
    n_orb = lax.axis_size("orb")
    vmem = pl.BlockSpec(memory_space=pltpu.VMEM)
    smem = pl.BlockSpec(memory_space=pltpu.SMEM)
    f32 = jnp.float32
    slab = pltpu.VMEM((cells, planes, width), f32)

    orbital = jnp.transpose(orbitals[0], (1, 0, 2)).astype(f32)
    packed = jnp.concatenate([orbital, jnp.transpose(potential, (1, 0, 2))], 0)

    halo = -(-RADIUS * MAXDEG // cells)
    if n_dom <= 2 * halo + 1:
        pairs = [xor_pairs(n_dom, k) for k in range(1, n_dom)]
    else:
        pairs = [shift_pairs(n_dom, s * k) for k in range(1, halo + 1) for s in (1, -1)]
    panel = chain(degree, [packed] + [lax.ppermute(packed, "dom", p) for p in pairs], n_dom)

    coefficients = rotation[:, 0, 0].astype(f32)
    beside = lax.ppermute(coefficients, "orb", xor_pairs(n_orb, 1))
    masks = sorted(range(2, n_orb, 2), key=lambda m: -m)
    panels = [panel] + [lax.ppermute(panel, "orb", xor_pairs(n_orb, m)) for m in masks]
    mine, theirs = pl.pallas_call(
        functools.partial(combine_kernel, [0] + masks),
        out_shape=(slab, slab),
        in_specs=[smem] * 3 + [vmem] * len(panels),
        out_specs=(vmem, vmem),
    )(owners, coefficients, beside, *[in_vmem(p) for p in panels])
    rotated = mine + lax.ppermute(theirs, "orb", xor_pairs(n_orb, 1))
    return tuple(jnp.transpose(x, (1, 0, 2))[None] for x in (panel, rotated))


def solution(mesh):
    placed = (
        P("orb", None, "dom", None),
        P(None, "dom", None),
        P("orb"),
        P(),
        P(None, None, "orb"),
    )
    return jax.shard_map(
        per_device,
        mesh=mesh,
        in_specs=placed,
        out_specs=(P("orb", None, "dom", None), P("orb", None, "dom", None)),
        check_vma=False,
    )
```

```python
import functools

import jax
import jax.numpy as jnp
import ml_dtypes
import numpy as np
from jax import lax
from jax.experimental import pallas as pl
from jax.experimental.pallas import tpu as pltpu
from jax.sharding import PartitionSpec as P

RADIUS = 6
MAXDEG = 8
STEPS = 4

STENCIL = (
    -5369.0 / 1800.0,
    12.0 / 7.0,
    -15.0 / 56.0,
    10.0 / 189.0,
    -1.0 / 112.0,
    2.0 / 1925.0,
    -1.0 / 16632.0,
)
FILTER_CENTER = 7.75
FILTER_HALF = 6.25
SCALE = 2.0 / FILTER_HALF
TAPS = tuple(-0.5 * SCALE * c for c in STENCIL[1:])
DIAGONAL = SCALE * (-1.5 * STENCIL[0] - FILTER_CENTER)


def xor_pairs(count, mask):
    return [(i, i ^ mask) for i in range(count)]


def shift_pairs(count, step):
    return [(i, i - step) for i in range(count) if 0 <= i - step < count]


def split(values):
    high = values.astype(jnp.bfloat16)
    return high, (values - high.astype(jnp.float32)).astype(jnp.bfloat16)


def ring(count, copies):
    matrix = np.zeros((count, count), np.float64)
    for k, tap in enumerate(TAPS, 1):
        for i in range(count):
            matrix[i, (i + k) % count] += tap
            matrix[i, (i - k) % count] += tap
    matrix = np.kron(np.eye(copies), matrix)
    high = matrix.astype(ml_dtypes.bfloat16)
    low = (matrix - high.astype(np.float64)).astype(ml_dtypes.bfloat16)
    return high, low


def chain_kernel(whole, slots, groups, n_dom, degree_ref, rows_ref, *refs):
    planes_at = dict(zip(groups, refs))
    refs = refs[len(groups) :]
    blocks = refs[: len(slots)]
    out_ref, *fields, potential = refs[len(slots) :]
    cells = blocks[0].shape[0] // 2
    planes, width = potential.shape[1:]
    window = potential.shape[0]
    degree = degree_ref[0]
    dom = lax.axis_index("dom")
    home = dom if whole else window // cells // 2
    starts = [(dom ^ k if whole else home + k) * cells for k in slots]

    for start, block in zip(starts, blocks):
        potential[pl.ds(start, cells)] = SCALE * block[cells:] + DIAGONAL
    for ref in fields:
        ref[pl.ds(0, RADIUS)] = jnp.zeros((RADIUS, planes, width), jnp.float32)
        ref[pl.ds(RADIUS + window, RADIUS)] = jnp.zeros((RADIUS, planes, width), jnp.float32)

    def begin(current, previous):
        for start, block in zip(starts, blocks):
            current[pl.ds(RADIUS + start, cells)] = block[:cells]
        previous[pl.ds(RADIUS, window)] = jnp.zeros((window, planes, width), jnp.float32)

    pl.when(degree % 2 == 0)(functools.partial(begin, fields[0], fields[1]))
    pl.when(degree % 2 == 1)(functools.partial(begin, fields[1], fields[0]))

    def advance(parity, factor, base, extent):
        source, target = fields[1 - parity], fields[parity]
        high, low = split(source[pl.ds(RADIUS + base, extent)].reshape(extent * planes, width))
        both = jnp.concatenate([high, low], 1)
        across = jnp.dot(both, rows_ref[...], preferred_element_type=jnp.float32)
        group = max(m for m in planes_at if extent % (2 * m) == 0)
        size = group * planes
        alongs = []
        for top in range(0, extent * planes, 2 * size):
            pieces = [jnp.concatenate([v[top : top + size], v[top + size : top + 2 * size]], 1) for v in (high, low)]
            alongs.append(
                jnp.dot(
                    planes_at[group][...], jnp.concatenate(pieces, 0), preferred_element_type=jnp.float32
                )
            )
        for part in range(0, extent, RADIUS):
            x = base + part
            near = source[pl.ds(x, 3 * RADIUS)]
            total = potential[pl.ds(x, RADIUS)] * near[RADIUS : 2 * RADIUS]
            for k in range(1, RADIUS + 1):
                beside = near[RADIUS + k : 2 * RADIUS + k] + near[RADIUS - k : 2 * RADIUS - k]
                total = total + TAPS[k - 1] * beside
            spot = pl.ds(RADIUS + x, RADIUS)
            target[spot] = factor * total - target[spot]
        for index, along in enumerate(alongs):
            along = along[:size] + along[size:]
            for half in range(2):
                top = (2 * index + half) * size
                plane_sum = across[top : top + size, :width] + across[top : top + size, width:]
                plane_sum = plane_sum + along[:, half * width : (half + 1) * width]
                spot = pl.ds(RADIUS + base + (2 * index + half) * group, group)
                target[spot] = target[spot] + factor * plane_sum.reshape(group, planes, width)

    def level(left, parity, reach):
        factor = jnp.where(left == degree - 1, 0.5, 1.0)
        if whole:
            extent = min(cells + 2 * reach, window)
            advance(parity, factor, jnp.clip(home * cells - reach, 0, window - extent), extent)
            return
        for block in range(home - -(-reach // cells), home + -(-reach // cells) + 1):
            place = dom + block - home
            pl.when((place >= 0) & (place < n_dom))(functools.partial(advance, parity, factor, block * cells, cells))

    def levels(fewest, most, reach):
        top = jnp.minimum(most, degree - 1)
        parity = fewest % 2

        def pair(index, carry):
            left = fewest + 2 * (count // 2 - index) - 1
            level(left, 1 - parity, reach)
            level(left - 1, parity, reach)
            return carry

        count = jnp.maximum(top - fewest + 1, 0)
        if most > fewest:
            pl.when(count % 2 == 1)(lambda: level(top, parity, reach))
            lax.fori_loop(0, count // 2, pair, 0)
        else:
            pl.when(count == 1)(lambda: level(fewest, parity, reach))

    bounds = [RADIUS * left for left in range(MAXDEG)]
    if whole:
        bounds = [min(reach, (window - cells + 1) // 2) for reach in bounds]
    for reach in sorted(set(bounds), reverse=True):
        lefts = [left for left in range(MAXDEG) if bounds[left] == reach]
        levels(lefts[0], lefts[-1], reach)
    out_ref[...] = fields[0][pl.ds(RADIUS + home * cells, cells)]


def combine_kernel(count, weights_ref, *refs):
    panels, outs = refs[:count], refs[count:]
    for out, ref in enumerate(outs):
        total = None
        for index, panel in enumerate(panels):
            term = weights_ref[out, index : index + 1] * panel[...]
            total = term if total is None else total + term
        ref[...] = total


def in_vmem(x):
    return pltpu.with_memory_space_constraint(x, pltpu.VMEM)


def chain(degree, blocks, n_dom):
    cells, planes, width = blocks[0].shape[0] // 2, *blocks[0].shape[1:]
    halo = -(-RADIUS * MAXDEG // cells)
    whole = n_dom <= 2 * halo + 1
    if whole:
        slots = list(range(n_dom))
        window = n_dom * cells
        extents = {min(cells + 2 * RADIUS * left, window) for left in range(MAXDEG)}
    else:
        slots = [0] + [s * k for k in range(1, halo + 1) for s in (1, -1)]
        window = (2 * halo + 1) * cells
        extents = {cells}
    high, low = ring(width, 1)
    across = np.block([[high, low], [high, low]])
    groups = sorted({max(g for g in range(1, width // planes + 1) if e % (2 * g) == 0) for e in extents})
    alongs = [np.block([[m, m] for m in ring(planes, g)]) for g in groups]
    field = pltpu.VMEM((window + 2 * RADIUS, planes, width), jnp.float32)
    vmem = pl.BlockSpec(memory_space=pltpu.VMEM)
    smem = pl.BlockSpec(memory_space=pltpu.SMEM)
    operands = [jnp.asarray(m) for m in [across] + alongs] + blocks
    return pl.pallas_call(
        functools.partial(chain_kernel, whole, slots, groups, n_dom),
        out_shape=pltpu.VMEM((cells, planes, width), jnp.float32),
        in_specs=[smem] + [vmem] * len(operands),
        out_specs=vmem,
        scratch_shapes=[field, field, pltpu.VMEM((window, planes, width), jnp.float32)],
    )(degree, *[in_vmem(x) for x in operands])


def per_device(orbitals, potential, degree, owners, rotation):
    _, planes, cells, width = orbitals.shape
    n_dom = lax.axis_size("dom")
    n_orb = lax.axis_size("orb")
    me = lax.axis_index("orb")
    vmem = pl.BlockSpec(memory_space=pltpu.VMEM)
    f32 = jnp.float32
    slab = pltpu.VMEM((cells, planes, width), f32)

    orbital = jnp.transpose(orbitals[0], (1, 0, 2)).astype(f32)
    potential = jnp.transpose(potential, (1, 0, 2))
    packed = jnp.concatenate([orbital, potential], 0)
    halo = -(-RADIUS * MAXDEG // cells)
    if n_dom <= 2 * halo + 1:
        pairs = [xor_pairs(n_dom, k) for k in range(1, n_dom)]
    else:
        pairs = [shift_pairs(n_dom, s * k) for k in range(1, halo + 1) for s in (1, -1)]
    arrived = [lax.ppermute(packed, "dom", p) for p in pairs]
    panel = chain(degree, [packed] + arrived, n_dom)

    coefficients = rotation[:, 0, 0].astype(f32)
    beside = lax.ppermute(coefficients, "orb", xor_pairs(n_orb, 1))
    masks = sorted(range(2, n_orb, 2), key=lambda m: (m % 4 == 2, m))
    panels = [panel] + [lax.ppermute(panel, "orb", xor_pairs(n_orb, m)) for m in masks]
    held = jnp.stack([me ^ m for m in [0] + masks])
    chosen = (owners[:, None] == held[None, :]).astype(f32)
    weights = jnp.stack([jnp.sum(c[:, None] * chosen, 0) for c in (coefficients, beside)])
    weights = jnp.broadcast_to(weights[:, :, None], weights.shape + (width,))
    mine, theirs = pl.pallas_call(
        functools.partial(combine_kernel, len(panels)),
        out_shape=(slab, slab),
        in_specs=[vmem] * (1 + len(panels)),
        out_specs=(vmem, vmem),
    )(in_vmem(weights), *[in_vmem(p) for p in panels])
    rotated = mine + lax.ppermute(theirs, "orb", xor_pairs(n_orb, 1))
    return tuple(jnp.transpose(x, (1, 0, 2))[None] for x in (panel, rotated))


def solution(mesh):
    placed = (
        P("orb", None, "dom", None),
        P(None, "dom", None),
        P("orb"),
        P(),
        P(None, None, "orb"),
    )
    return jax.shard_map(
        per_device,
        mesh=mesh,
        in_specs=placed,
        out_specs=(P("orb", None, "dom", None), P("orb", None, "dom", None)),
        check_vma=False,
    )
```

```python
import functools

import jax
import jax.numpy as jnp
import ml_dtypes
import numpy as np
from jax import lax
from jax.experimental import pallas as pl
from jax.experimental.pallas import tpu as pltpu
from jax.sharding import PartitionSpec as P

RADIUS = 6
MAXDEG = 8
STEPS = 4

STENCIL = (
    -5369.0 / 1800.0,
    12.0 / 7.0,
    -15.0 / 56.0,
    10.0 / 189.0,
    -1.0 / 112.0,
    2.0 / 1925.0,
    -1.0 / 16632.0,
)
FILTER_CENTER = 7.75
FILTER_HALF = 6.25
SCALE = 2.0 / FILTER_HALF
TAPS = tuple(-0.5 * SCALE * c for c in STENCIL[1:])
DIAGONAL = SCALE * (-1.5 * STENCIL[0] - FILTER_CENTER)


def xor_pairs(count, mask):
    return [(i, i ^ mask) for i in range(count)]


def shift_pairs(count, step):
    return [(i, i - step) for i in range(count) if 0 <= i - step < count]


def split(values):
    high = values.astype(jnp.bfloat16)
    return high, (values - high.astype(jnp.float32)).astype(jnp.bfloat16)


def stencil(count, cells):
    around = np.zeros((count, count), np.float64)
    for k, tap in enumerate(TAPS, 1):
        for i in range(count):
            around[i, (i + k) % count] += tap
            around[i, (i - k) % count] += tap
    between = sum(tap * (np.eye(cells, k=k) + np.eye(cells, k=-k)) for k, tap in enumerate(TAPS, 1))
    matrix = np.kron(np.eye(cells), around) + np.kron(between, np.eye(count))
    high = matrix.astype(ml_dtypes.bfloat16)
    low = (matrix - high.astype(np.float64)).astype(ml_dtypes.bfloat16)
    return high, low


def chain_kernel(whole, slots, groups, n_dom, degree_ref, rows_ref, *refs):
    planes_at = dict(zip(groups, refs))
    refs = refs[len(groups) :]
    blocks = refs[: len(slots)]
    out_ref, *fields, potential = refs[len(slots) :]
    cells = blocks[0].shape[0] // 2
    planes, width = potential.shape[1:]
    window = potential.shape[0]
    degree = degree_ref[0]
    dom = lax.axis_index("dom")
    home = dom if whole else window // cells // 2
    starts = [(dom ^ k if whole else home + k) * cells for k in slots]

    for start, block in zip(starts, blocks):
        potential[pl.ds(start, cells)] = SCALE * block[cells:] + DIAGONAL
    for ref in fields:
        ref[pl.ds(0, RADIUS)] = jnp.zeros((RADIUS, planes, width), jnp.float32)
        ref[pl.ds(RADIUS + window, RADIUS)] = jnp.zeros((RADIUS, planes, width), jnp.float32)

    def begin(current, previous):
        for start, block in zip(starts, blocks):
            current[pl.ds(RADIUS + start, cells)] = block[:cells]
        previous[pl.ds(RADIUS, window)] = jnp.zeros((window, planes, width), jnp.float32)

    pl.when(degree % 2 == 0)(functools.partial(begin, fields[0], fields[1]))
    pl.when(degree % 2 == 1)(functools.partial(begin, fields[1], fields[0]))

    def advance(parity, factor, base, extent):
        source, target = fields[1 - parity], fields[parity]
        high, low = split(source[pl.ds(RADIUS + base, extent)].reshape(extent * planes, width))
        both = jnp.concatenate([high, low], 1)
        across = jnp.dot(both, rows_ref[...], preferred_element_type=jnp.float32)
        group = max(m for m in planes_at if extent % (2 * m) == 0)
        size = group * planes
        alongs = []
        for top in range(0, extent * planes, 2 * size):
            pieces = [jnp.concatenate([v[top : top + size], v[top + size : top + 2 * size]], 1) for v in (high, low)]
            alongs.append(
                jnp.dot(
                    planes_at[group][...], jnp.concatenate(pieces, 0), preferred_element_type=jnp.float32
                )
            )
        for tile in range(0, extent, group):
            x = RADIUS + base + tile
            below = [source[x - RADIUS + j] for j in range(RADIUS)]
            above = [source[x + group + j] for j in range(RADIUS)]
            for i in range(group):
                total = potential[x - RADIUS + i] * source[x + i] - target[x + i]
                for k in range(1, RADIUS + 1):
                    outside = ([below[RADIUS + i - k]] if i < k else []) + ([above[i + k - group]] if i + k >= group else [])
                    if outside:
                        total = total + TAPS[k - 1] * functools.reduce(jnp.add, outside)
                target[x + i] = total
        for index, along in enumerate(alongs):
            along = along[:size] + along[size:]
            for half in range(2):
                top = (2 * index + half) * size
                plane_sum = across[top : top + size, :width] + across[top : top + size, width:]
                plane_sum = plane_sum + along[:, half * width : (half + 1) * width]
                spot = pl.ds(RADIUS + base + (2 * index + half) * group, group)
                target[spot] = factor * (target[spot] + plane_sum.reshape(group, planes, width))

    def level(left, parity, reach):
        factor = jnp.where(left == degree - 1, 0.5, 1.0)
        if whole:
            extent = min(cells + 2 * reach, window)
            advance(parity, factor, jnp.clip(home * cells - reach, 0, window - extent), extent)
            return
        for block in range(home - -(-reach // cells), home + -(-reach // cells) + 1):
            place = dom + block - home
            pl.when((place >= 0) & (place < n_dom))(functools.partial(advance, parity, factor, block * cells, cells))

    def levels(fewest, most, reach):
        top = jnp.minimum(most, degree - 1)
        parity = fewest % 2

        def pair(index, carry):
            left = fewest + 2 * (count // 2 - index) - 1
            level(left, 1 - parity, reach)
            level(left - 1, parity, reach)
            return carry

        count = jnp.maximum(top - fewest + 1, 0)
        if most > fewest:
            pl.when(count % 2 == 1)(lambda: level(top, parity, reach))
            lax.fori_loop(0, count // 2, pair, 0)
        else:
            pl.when(count == 1)(lambda: level(fewest, parity, reach))

    bounds = [RADIUS * left for left in range(MAXDEG)]
    if whole:
        bounds = [min(reach, (window - cells + 1) // 2) for reach in bounds]
    for reach in sorted(set(bounds), reverse=True):
        lefts = [left for left in range(MAXDEG) if bounds[left] == reach]
        levels(lefts[0], lefts[-1], reach)
    out_ref[...] = fields[0][pl.ds(RADIUS + home * cells, cells)]


def combine_kernel(count, weights_ref, *refs):
    panels, outs = refs[:count], refs[count:]
    for out, ref in enumerate(outs):
        total = None
        for index, panel in enumerate(panels):
            term = weights_ref[out, index : index + 1] * panel[...]
            total = term if total is None else total + term
        ref[...] = total


def in_vmem(x):
    return pltpu.with_memory_space_constraint(x, pltpu.VMEM)


def chain(degree, blocks, n_dom):
    cells, planes, width = blocks[0].shape[0] // 2, *blocks[0].shape[1:]
    halo = -(-RADIUS * MAXDEG // cells)
    whole = n_dom <= 2 * halo + 1
    if whole:
        slots = list(range(n_dom))
        window = n_dom * cells
        extents = {min(cells + 2 * RADIUS * left, window) for left in range(MAXDEG)}
    else:
        slots = [0] + [s * k for k in range(1, halo + 1) for s in (1, -1)]
        window = (2 * halo + 1) * cells
        extents = {cells}
    high, low = stencil(width, 1)
    across = np.block([[high, low], [high, low]])
    groups = sorted({max(g for g in range(1, width // planes + 1) if e % (2 * g) == 0) for e in extents})
    alongs = [np.block([[m, m] for m in stencil(planes, g)]) for g in groups]
    field = pltpu.VMEM((window + 2 * RADIUS, planes, width), jnp.float32)
    vmem = pl.BlockSpec(memory_space=pltpu.VMEM)
    smem = pl.BlockSpec(memory_space=pltpu.SMEM)
    operands = [jnp.asarray(m) for m in [across] + alongs] + blocks
    return pl.pallas_call(
        functools.partial(chain_kernel, whole, slots, groups, n_dom),
        out_shape=pltpu.VMEM((cells, planes, width), jnp.float32),
        in_specs=[smem] + [vmem] * len(operands),
        out_specs=vmem,
        scratch_shapes=[field, field, pltpu.VMEM((window, planes, width), jnp.float32)],
    )(degree, *[in_vmem(x) for x in operands])


def per_device(orbitals, potential, degree, owners, rotation):
    _, planes, cells, width = orbitals.shape
    n_dom = lax.axis_size("dom")
    n_orb = lax.axis_size("orb")
    me = lax.axis_index("orb")
    vmem = pl.BlockSpec(memory_space=pltpu.VMEM)
    f32 = jnp.float32
    slab = pltpu.VMEM((cells, planes, width), f32)

    orbital = jnp.transpose(orbitals[0], (1, 0, 2)).astype(f32)
    potential = jnp.transpose(potential, (1, 0, 2))
    packed = jnp.concatenate([orbital, potential], 0)
    halo = -(-RADIUS * MAXDEG // cells)
    if n_dom <= 2 * halo + 1:
        pairs = [xor_pairs(n_dom, k) for k in range(1, n_dom)]
    else:
        pairs = [shift_pairs(n_dom, s * k) for k in range(1, halo + 1) for s in (1, -1)]
    arrived = [lax.ppermute(packed, "dom", p) for p in pairs]
    panel = chain(degree, [packed] + arrived, n_dom)

    coefficients = rotation[:, 0, 0].astype(f32)
    beside = lax.ppermute(coefficients, "orb", xor_pairs(n_orb, 1))
    masks = sorted(range(2, n_orb, 2), key=lambda m: (m % 4 == 2, m))
    panels = [panel] + [lax.ppermute(panel, "orb", xor_pairs(n_orb, m)) for m in masks]
    held = jnp.stack([me ^ m for m in [0] + masks])
    chosen = (owners[:, None] == held[None, :]).astype(f32)
    weights = jnp.stack([jnp.sum(c[:, None] * chosen, 0) for c in (coefficients, beside)])
    weights = jnp.broadcast_to(weights[:, :, None], weights.shape + (width,))
    mine, theirs = pl.pallas_call(
        functools.partial(combine_kernel, len(panels)),
        out_shape=(slab, slab),
        in_specs=[vmem] * (1 + len(panels)),
        out_specs=(vmem, vmem),
    )(in_vmem(weights), *[in_vmem(p) for p in panels])
    rotated = mine + lax.ppermute(theirs, "orb", xor_pairs(n_orb, 1))
    return tuple(jnp.transpose(x, (1, 0, 2))[None] for x in (panel, rotated))


def solution(mesh):
    placed = (
        P("orb", None, "dom", None),
        P(None, "dom", None),
        P("orb"),
        P(),
        P(None, None, "orb"),
    )
    return jax.shard_map(
        per_device,
        mesh=mesh,
        in_specs=placed,
        out_specs=(P("orb", None, "dom", None), P("orb", None, "dom", None)),
        check_vma=False,
    )
```

```python
import functools

import jax
import jax.numpy as jnp
import ml_dtypes
import numpy as np
from jax import lax
from jax.experimental import pallas as pl
from jax.experimental.pallas import tpu as pltpu
from jax.sharding import PartitionSpec as P

RADIUS = 6
MAXDEG = 8
STEPS = 4

STENCIL = (
    -5369.0 / 1800.0,
    12.0 / 7.0,
    -15.0 / 56.0,
    10.0 / 189.0,
    -1.0 / 112.0,
    2.0 / 1925.0,
    -1.0 / 16632.0,
)
FILTER_CENTER = 7.75
FILTER_HALF = 6.25
SCALE = 2.0 / FILTER_HALF
TAPS = tuple(-0.5 * SCALE * c for c in STENCIL[1:])
DIAGONAL = SCALE * (-1.5 * STENCIL[0] - FILTER_CENTER)


def xor_pairs(count, mask):
    return [(i, i ^ mask) for i in range(count)]


def shift_pairs(count, step):
    return [(i, i - step) for i in range(count) if 0 <= i - step < count]


def split(values):
    high = values.astype(jnp.bfloat16)
    return high, (values - high.astype(jnp.float32)).astype(jnp.bfloat16)


def stencil(count, cells):
    around = np.zeros((count, count), np.float64)
    for k, tap in enumerate(TAPS, 1):
        for i in range(count):
            around[i, (i + k) % count] += tap
            around[i, (i - k) % count] += tap
    between = sum(tap * (np.eye(cells, k=k) + np.eye(cells, k=-k)) for k, tap in enumerate(TAPS, 1))
    matrix = np.kron(np.eye(cells), around) + np.kron(between, np.eye(count))
    high = matrix.astype(ml_dtypes.bfloat16)
    low = (matrix - high.astype(np.float64)).astype(ml_dtypes.bfloat16)
    return high, low


class Layout:
    def __init__(self, n_dom, cells, planes, width):
        self.n_dom, self.cells, self.planes, self.width = n_dom, cells, planes, width
        halo = -(-RADIUS * MAXDEG // cells)
        self.whole = n_dom <= 2 * halo + 1
        if self.whole:
            self.slots = list(range(1, n_dom))
            self.pairs = [xor_pairs(n_dom, k) for k in self.slots]
            self.window = n_dom * cells
            extents = {min(cells + 2 * RADIUS * left, self.window) for left in range(MAXDEG)}
        else:
            self.slots = [s * k for k in range(1, halo + 1) for s in (1, -1)]
            self.pairs = [shift_pairs(n_dom, k) for k in self.slots]
            self.window = (2 * halo + 1) * cells
            extents = {cells}
        self.groups = sorted({max(g for g in range(1, width // planes + 1) if e % (2 * g) == 0) for e in extents})
        high, low = stencil(width, 1)
        across = np.block([[high, low], [high, low]])
        self.matrices = [across] + [np.block([[m, m] for m in stencil(planes, g)]) for g in self.groups]

    def home(self):
        return lax.axis_index("dom") if self.whole else self.window // self.cells // 2

    def starts(self):
        home = self.home()
        return [(home ^ k if self.whole else home + k) * self.cells for k in [0] + self.slots]

    def on_grid(self, reach, act):
        home, dom = self.home(), lax.axis_index("dom")
        for block in range(home - reach, home + reach + 1):
            place = dom + block - home
            pl.when((place >= 0) & (place < self.n_dom))(functools.partial(act, block))


def apply_taps(layout, matrices, source, target, shift, base, extent, begin):
    planes, width = layout.planes, layout.width
    high, low = split(source[pl.ds(RADIUS + base, extent)].reshape(extent * planes, width))
    across = jnp.dot(jnp.concatenate([high, low], 1), matrices[0][...], preferred_element_type=jnp.float32)
    group = max(m for m in layout.groups if extent % (2 * m) == 0)
    size = group * planes
    alongs = []
    for top in range(0, extent * planes, 2 * size):
        pieces = [jnp.concatenate([v[top : top + size], v[top + size : top + 2 * size]], 1) for v in (high, low)]
        matrix = matrices[1 + layout.groups.index(group)]
        alongs.append(jnp.dot(matrix[...], jnp.concatenate(pieces, 0), preferred_element_type=jnp.float32))
    for tile in range(0, extent, group):
        x = RADIUS + base + tile
        below = [source[x - RADIUS + j] for j in range(RADIUS)]
        above = [source[x + group + j] for j in range(RADIUS)]
        for i in range(group):
            terms = begin(base + tile + i)
            for k in range(1, RADIUS + 1):
                outside = ([below[RADIUS + i - k]] if i < k else []) + ([above[i + k - group]] if i + k >= group else [])
                if outside:
                    terms.append(TAPS[k - 1] * functools.reduce(jnp.add, outside))
            target[shift + base + tile + i] = functools.reduce(jnp.add, terms)
    for index, along in enumerate(alongs):
        along = along[:size] + along[size:]
        for half in range(2):
            top = (2 * index + half) * size
            plane_sum = across[top : top + size, :width] + across[top : top + size, width:]
            plane_sum = plane_sum + along[:, half * width : (half + 1) * width]
            spot = pl.ds(shift + base + (2 * index + half) * group, group)
            target[spot] = target[spot] + plane_sum.reshape(group, planes, width)


def open_kernel(layout, *refs):
    count = len(layout.matrices)
    matrices, blocks, (start_ref, taps_ref) = refs[:count], refs[count:-2], refs[-2:]
    cells, window = layout.cells, layout.window
    edge = jnp.zeros((RADIUS, layout.planes, layout.width), jnp.float32)
    start_ref[pl.ds(0, RADIUS)] = edge
    start_ref[pl.ds(RADIUS + window, RADIUS)] = edge
    for start, block in zip(layout.starts(), blocks):
        start_ref[pl.ds(RADIUS + start, cells)] = block[:cells]

    def act(base, extent):
        apply_taps(layout, matrices, start_ref, taps_ref, 0, base, extent, lambda x: [])

    if layout.whole:
        act(0, window)
    else:
        taps_ref[...] = jnp.zeros(taps_ref.shape, jnp.float32)
        layout.on_grid(window // cells // 2, lambda block: act(block * cells, cells))


def chain_kernel(layout, degree_ref, *refs):
    count = len(layout.matrices)
    matrices, (own_ref, swapped_ref, start_ref, taps_ref), refs = refs[:count], refs[count : count + 4], refs[count + 4 :]
    blocks, (out_ref, *fields, potential) = refs[: len(layout.slots)], refs[len(layout.slots) :]
    cells, window = layout.cells, layout.window
    half = cells // 2
    core = lax.axis_index("orb") % 2
    degree = degree_ref[0]
    home = layout.home()

    starts = layout.starts()
    potential[pl.ds(starts[0], cells)] = SCALE * own_ref[...] + DIAGONAL
    for index, (start, block) in enumerate(zip(starts[1:], blocks)):
        potential[pl.ds(start + core * half, half)] = SCALE * block[cells:] + DIAGONAL
        other = swapped_ref[index * half : (index + 1) * half]
        potential[pl.ds(start + (1 - core) * half, half)] = SCALE * other + DIAGONAL

    def begin(current, previous):
        previous[...] = start_ref[...]
        current[pl.ds(0, RADIUS)] = start_ref[pl.ds(0, RADIUS)]
        current[pl.ds(RADIUS + window, RADIUS)] = start_ref[pl.ds(RADIUS + window, RADIUS)]
        for x in range(0, window, RADIUS):
            here = pl.ds(RADIUS + x, RADIUS)
            current[here] = 0.5 * (taps_ref[pl.ds(x, RADIUS)] + potential[pl.ds(x, RADIUS)] * start_ref[here])

    pl.when(degree % 2 == 1)(functools.partial(begin, fields[0], fields[1]))
    pl.when(degree % 2 == 0)(functools.partial(begin, fields[1], fields[0]))

    def level(parity, reach):
        source, target = fields[1 - parity], fields[parity]

        def act(base, extent):
            def first(x):
                return [potential[x] * source[RADIUS + x] - target[RADIUS + x]]

            apply_taps(layout, matrices, source, target, RADIUS, base, extent, first)

        if layout.whole:
            extent = min(cells + 2 * reach, window)
            act(jnp.clip(home * cells - reach, 0, window - extent), extent)
        else:
            layout.on_grid(-(-reach // cells), lambda block: act(block * cells, cells))

    def levels(fewest, most, reach):
        parity = fewest % 2
        total = jnp.maximum(jnp.minimum(most, degree - 2) - fewest + 1, 0)

        def pair(index, carry):
            level(1 - parity, reach)
            level(parity, reach)
            return carry

        pl.when(total % 2 == 1)(lambda: level(parity, reach))
        if most > fewest:
            lax.fori_loop(0, total // 2, pair, 0)

    bounds = [RADIUS * left for left in range(MAXDEG - 1)]
    if layout.whole:
        bounds = [min(reach, (window - cells + 1) // 2) for reach in bounds]
    for reach in sorted(set(bounds), reverse=True):
        lefts = [left for left in range(MAXDEG - 1) if bounds[left] == reach]
        levels(lefts[0], lefts[-1], reach)
    out_ref[...] = fields[0][pl.ds(RADIUS + home * cells, cells)]


def combine_kernel(count, weights_ref, *refs):
    panels, outs = refs[:count], refs[count:]
    for out, ref in enumerate(outs):
        total = None
        for index, panel in enumerate(panels):
            term = weights_ref[out, index : index + 1] * panel[...]
            total = term if total is None else total + term
        ref[...] = total


def in_vmem(x):
    return pltpu.with_memory_space_constraint(x, pltpu.VMEM)


def per_device(orbitals, potential, degree, owners, rotation):
    _, planes, cells, width = orbitals.shape
    n_orb = lax.axis_size("orb")
    me = lax.axis_index("orb")
    layout = Layout(lax.axis_size("dom"), cells, planes, width)
    vmem = pl.BlockSpec(memory_space=pltpu.VMEM)
    smem = pl.BlockSpec(memory_space=pltpu.SMEM)
    f32 = jnp.float32
    slab = pltpu.VMEM((cells, planes, width), f32)
    window = pltpu.VMEM((layout.window, planes, width), f32)
    padded = pltpu.VMEM((layout.window + 2 * RADIUS, planes, width), f32)

    orbital = jnp.transpose(orbitals[0], (1, 0, 2)).astype(f32)
    potential = jnp.transpose(potential, (1, 0, 2))
    half = lax.dynamic_slice_in_dim(potential, me % 2 * (cells // 2), cells // 2, 0)
    packed = jnp.concatenate([orbital, half], 0)
    arrived = [lax.ppermute(packed, "dom", p) for p in layout.pairs]
    coefficients = jnp.pad(rotation[:, 0, 0].astype(f32), (0, planes - STEPS))
    coefficients = jnp.broadcast_to(coefficients[None, :, None], (1, planes, width))
    swapped = jnp.concatenate([a[cells:] for a in arrived] + [coefficients], 0)
    swapped = lax.ppermute(swapped, "orb", xor_pairs(n_orb, 1))

    matrices = [in_vmem(jnp.asarray(m)) for m in layout.matrices]
    operands = matrices + [in_vmem(x) for x in [packed] + arrived]
    start, taps = pl.pallas_call(
        functools.partial(open_kernel, layout),
        out_shape=(padded, window),
        in_specs=[vmem] * len(operands),
        out_specs=(vmem, vmem),
    )(*operands)
    operands = matrices + [in_vmem(x) for x in [potential, swapped, start, taps] + arrived]
    panel = pl.pallas_call(
        functools.partial(chain_kernel, layout),
        out_shape=slab,
        in_specs=[smem] + [vmem] * len(operands),
        out_specs=vmem,
        scratch_shapes=[padded, padded, window],
    )(degree, *operands)

    masks = sorted(range(2, n_orb, 2), key=lambda m: (m % 4 == 2, m))
    panels = [panel] + [lax.ppermute(panel, "orb", xor_pairs(n_orb, m)) for m in masks]
    held = jnp.stack([me ^ m for m in [0] + masks])
    chosen = (owners[:, None] == held[None, :]).astype(f32)
    columns = jnp.stack([coefficients[0, :STEPS], swapped[-1, :STEPS]])
    weights = jnp.sum(columns[:, :, None, :] * chosen[None, :, :, None], 1)
    mine, theirs = pl.pallas_call(
        functools.partial(combine_kernel, len(panels)),
        out_shape=(slab, slab),
        in_specs=[vmem] * (1 + len(panels)),
        out_specs=(vmem, vmem),
    )(in_vmem(weights), *[in_vmem(p) for p in panels])
    rotated = mine + lax.ppermute(theirs, "orb", xor_pairs(n_orb, 1))
    return tuple(jnp.transpose(x, (1, 0, 2))[None] for x in (panel, rotated))


def solution(mesh):
    placed = (
        P("orb", None, "dom", None),
        P(None, "dom", None),
        P("orb"),
        P(),
        P(None, None, "orb"),
    )
    return jax.shard_map(
        per_device,
        mesh=mesh,
        in_specs=placed,
        out_specs=(P("orb", None, "dom", None), P("orb", None, "dom", None)),
        check_vma=False,
    )
```

```python
import functools

import jax
import jax.numpy as jnp
import ml_dtypes
import numpy as np
from jax import lax
from jax.experimental import pallas as pl
from jax.experimental.pallas import tpu as pltpu
from jax.sharding import PartitionSpec as P

RADIUS = 6
MAXDEG = 8
STEPS = 4

STENCIL = (
    -5369.0 / 1800.0,
    12.0 / 7.0,
    -15.0 / 56.0,
    10.0 / 189.0,
    -1.0 / 112.0,
    2.0 / 1925.0,
    -1.0 / 16632.0,
)
FILTER_CENTER = 7.75
FILTER_HALF = 6.25
SCALE = 2.0 / FILTER_HALF
TAPS = tuple(-0.5 * SCALE * c for c in STENCIL[1:])
DIAGONAL = SCALE * (-1.5 * STENCIL[0] - FILTER_CENTER)


def xor_pairs(count, mask):
    return [(i, i ^ mask) for i in range(count)]


def shift_pairs(count, step):
    return [(i, i - step) for i in range(count) if 0 <= i - step < count]


def split(values):
    high = values.astype(jnp.bfloat16)
    return high, (values - high.astype(jnp.float32)).astype(jnp.bfloat16)


def stencil(count, cells):
    around = np.zeros((count, count), np.float64)
    for k, tap in enumerate(TAPS, 1):
        for i in range(count):
            around[i, (i + k) % count] += tap
            around[i, (i - k) % count] += tap
    between = sum(tap * (np.eye(cells, k=k) + np.eye(cells, k=-k)) for k, tap in enumerate(TAPS, 1))
    matrix = np.kron(np.eye(cells), around) + np.kron(between, np.eye(count))
    high = matrix.astype(ml_dtypes.bfloat16)
    low = (matrix - high.astype(np.float64)).astype(ml_dtypes.bfloat16)
    return high, low


class Layout:
    def __init__(self, n_dom, cells, planes, width):
        self.n_dom, self.cells, self.planes, self.width = n_dom, cells, planes, width
        halo = -(-RADIUS * MAXDEG // cells)
        self.whole = n_dom <= 2 * halo + 1
        if self.whole:
            self.slots = list(range(1, n_dom))
            self.pairs = [xor_pairs(n_dom, k) for k in self.slots]
            self.window = n_dom * cells
            extents = {min(cells + 2 * RADIUS * left, self.window) for left in range(MAXDEG)}
        else:
            self.slots = [s * k for k in range(1, halo + 1) for s in (1, -1)]
            self.pairs = [shift_pairs(n_dom, k) for k in self.slots]
            self.window = (2 * halo + 1) * cells
            extents = {cells}
        self.groups = sorted({max(g for g in range(1, width // planes + 1) if e % (2 * g) == 0) for e in extents})
        high, low = stencil(width, 1)
        across = np.block([[high, low], [high, low]])
        self.matrices = [across] + [np.block([[m, m] for m in stencil(planes, g)]) for g in self.groups]

    def home(self):
        return lax.axis_index("dom") if self.whole else self.window // self.cells // 2

    def starts(self):
        home = self.home()
        return [(home ^ k if self.whole else home + k) * self.cells for k in [0] + self.slots]

    def on_grid(self, reach, act):
        home, dom = self.home(), lax.axis_index("dom")
        for block in range(home - reach, home + reach + 1):
            place = dom + block - home
            pl.when((place >= 0) & (place < self.n_dom))(functools.partial(act, block))


def apply_taps(layout, matrices, source, target, shift, base, extent, begin):
    planes, width = layout.planes, layout.width
    high, low = split(source[pl.ds(RADIUS + base, extent)].reshape(extent * planes, width))
    across = jnp.dot(jnp.concatenate([high, low], 1), matrices[0][...], preferred_element_type=jnp.float32)
    group = max(m for m in layout.groups if extent % (2 * m) == 0)
    size = group * planes
    alongs = []
    for top in range(0, extent * planes, 2 * size):
        pieces = [jnp.concatenate([v[top : top + size], v[top + size : top + 2 * size]], 1) for v in (high, low)]
        matrix = matrices[1 + layout.groups.index(group)]
        alongs.append(jnp.dot(matrix[...], jnp.concatenate(pieces, 0), preferred_element_type=jnp.float32))
    for tile in range(0, extent, group):
        x = RADIUS + base + tile
        below = [source[x - RADIUS + j] for j in range(RADIUS)]
        above = [source[x + group + j] for j in range(RADIUS)]
        for i in range(group):
            terms = begin(base + tile + i)
            for k in range(1, RADIUS + 1):
                outside = ([below[RADIUS + i - k]] if i < k else []) + ([above[i + k - group]] if i + k >= group else [])
                if outside:
                    terms.append(TAPS[k - 1] * functools.reduce(jnp.add, outside))
            target[shift + base + tile + i] = functools.reduce(jnp.add, terms)
    for index, along in enumerate(alongs):
        along = along[:size] + along[size:]
        for half in range(2):
            top = (2 * index + half) * size
            plane_sum = across[top : top + size, :width] + across[top : top + size, width:]
            plane_sum = plane_sum + along[:, half * width : (half + 1) * width]
            spot = pl.ds(shift + base + (2 * index + half) * group, group)
            target[spot] = target[spot] + plane_sum.reshape(group, planes, width)


def halves_kernel(cells, coefficients_ref, *refs):
    *blocks, out_ref = refs
    half = cells // 2
    for index, block in enumerate(blocks):
        out_ref[pl.ds(index * half, half)] = block[cells:]
    out_ref[pl.ds(len(blocks) * half, 1)] = coefficients_ref[...]


def open_kernel(layout, *refs):
    count = len(layout.matrices)
    matrices, blocks, (start_ref, taps_ref) = refs[:count], refs[count:-2], refs[-2:]
    cells, window = layout.cells, layout.window
    edge = jnp.zeros((RADIUS, layout.planes, layout.width), jnp.float32)
    start_ref[pl.ds(0, RADIUS)] = edge
    start_ref[pl.ds(RADIUS + window, RADIUS)] = edge
    for start, block in zip(layout.starts(), blocks):
        start_ref[pl.ds(RADIUS + start, cells)] = block[:cells]

    def act(base, extent):
        apply_taps(layout, matrices, start_ref, taps_ref, 0, base, extent, lambda x: [])

    if layout.whole:
        act(0, window)
    else:
        taps_ref[...] = jnp.zeros(taps_ref.shape, jnp.float32)
        layout.on_grid(window // cells // 2, lambda block: act(block * cells, cells))


def chain_kernel(layout, degree_ref, *refs):
    count = len(layout.matrices)
    matrices, (own_ref, swapped_ref, start_ref, taps_ref), refs = refs[:count], refs[count : count + 4], refs[count + 4 :]
    blocks, (out_ref, *fields, potential) = refs[: len(layout.slots)], refs[len(layout.slots) :]
    cells, window = layout.cells, layout.window
    half = cells // 2
    core = lax.axis_index("orb") % 2
    degree = degree_ref[0]
    home = layout.home()

    starts = layout.starts()
    potential[pl.ds(starts[0], cells)] = SCALE * own_ref[...] + DIAGONAL
    for index, (start, block) in enumerate(zip(starts[1:], blocks)):
        potential[pl.ds(start + core * half, half)] = SCALE * block[cells:] + DIAGONAL
        other = swapped_ref[index * half : (index + 1) * half]
        potential[pl.ds(start + (1 - core) * half, half)] = SCALE * other + DIAGONAL

    def begin(current, previous):
        previous[...] = start_ref[...]
        current[pl.ds(0, RADIUS)] = start_ref[pl.ds(0, RADIUS)]
        current[pl.ds(RADIUS + window, RADIUS)] = start_ref[pl.ds(RADIUS + window, RADIUS)]
        for x in range(0, window, RADIUS):
            here = pl.ds(RADIUS + x, RADIUS)
            current[here] = 0.5 * (taps_ref[pl.ds(x, RADIUS)] + potential[pl.ds(x, RADIUS)] * start_ref[here])

    pl.when(degree % 2 == 1)(functools.partial(begin, fields[0], fields[1]))
    pl.when(degree % 2 == 0)(functools.partial(begin, fields[1], fields[0]))

    def level(parity, reach):
        source, target = fields[1 - parity], fields[parity]

        def act(base, extent):
            def first(x):
                return [potential[x] * source[RADIUS + x] - target[RADIUS + x]]

            apply_taps(layout, matrices, source, target, RADIUS, base, extent, first)

        if layout.whole:
            extent = min(cells + 2 * reach, window)
            act(jnp.clip(home * cells - reach, 0, window - extent), extent)
        else:
            layout.on_grid(-(-reach // cells), lambda block: act(block * cells, cells))

    def levels(fewest, most, reach):
        parity = fewest % 2
        total = jnp.maximum(jnp.minimum(most, degree - 2) - fewest + 1, 0)

        def pair(index, carry):
            level(1 - parity, reach)
            level(parity, reach)
            return carry

        pl.when(total % 2 == 1)(lambda: level(parity, reach))
        if most > fewest:
            lax.fori_loop(0, total // 2, pair, 0)

    bounds = [RADIUS * left for left in range(MAXDEG - 1)]
    if layout.whole:
        bounds = [min(reach, (window - cells + 1) // 2) for reach in bounds]
    for reach in sorted(set(bounds), reverse=True):
        lefts = [left for left in range(MAXDEG - 1) if bounds[left] == reach]
        levels(lefts[0], lefts[-1], reach)
    out_ref[...] = fields[0][pl.ds(RADIUS + home * cells, cells)]


def combine_kernel(count, weights_ref, *refs):
    panels, outs = refs[:count], refs[count:]
    for out, ref in enumerate(outs):
        total = None
        for index, panel in enumerate(panels):
            term = weights_ref[out, index : index + 1] * panel[...]
            total = term if total is None else total + term
        ref[...] = total


def in_vmem(x):
    return pltpu.with_memory_space_constraint(x, pltpu.VMEM)


def per_device(orbitals, potential, degree, owners, rotation):
    _, planes, cells, width = orbitals.shape
    n_orb = lax.axis_size("orb")
    me = lax.axis_index("orb")
    layout = Layout(lax.axis_size("dom"), cells, planes, width)
    vmem = pl.BlockSpec(memory_space=pltpu.VMEM)
    smem = pl.BlockSpec(memory_space=pltpu.SMEM)
    f32 = jnp.float32
    slab = pltpu.VMEM((cells, planes, width), f32)
    window = pltpu.VMEM((layout.window, planes, width), f32)
    padded = pltpu.VMEM((layout.window + 2 * RADIUS, planes, width), f32)

    orbital = jnp.transpose(orbitals[0], (1, 0, 2)).astype(f32)
    potential = jnp.transpose(potential, (1, 0, 2))
    half = lax.dynamic_slice_in_dim(potential, me % 2 * (cells // 2), cells // 2, 0)
    packed = jnp.concatenate([orbital, half], 0)
    arrived = [lax.ppermute(packed, "dom", p) for p in layout.pairs]
    coefficients = jnp.pad(rotation[:, 0, 0].astype(f32), (0, planes - STEPS))
    coefficients = jnp.broadcast_to(coefficients[None, :, None], (1, planes, width))
    halves = pl.pallas_call(
        functools.partial(halves_kernel, cells),
        out_shape=pltpu.VMEM((len(arrived) * (cells // 2) + 1, planes, width), f32),
        in_specs=[vmem] * (1 + len(arrived)),
        out_specs=vmem,
    )(*[in_vmem(x) for x in [coefficients] + arrived])
    swapped = lax.ppermute(halves, "orb", xor_pairs(n_orb, 1))

    matrices = [in_vmem(jnp.asarray(m)) for m in layout.matrices]
    operands = matrices + [in_vmem(x) for x in [packed] + arrived]
    start, taps = pl.pallas_call(
        functools.partial(open_kernel, layout),
        out_shape=(padded, window),
        in_specs=[vmem] * len(operands),
        out_specs=(vmem, vmem),
    )(*operands)
    operands = matrices + [in_vmem(x) for x in [potential, swapped, start, taps] + arrived]
    panel = pl.pallas_call(
        functools.partial(chain_kernel, layout),
        out_shape=slab,
        in_specs=[smem] + [vmem] * len(operands),
        out_specs=vmem,
        scratch_shapes=[padded, padded, window],
    )(degree, *operands)

    *near, last = sorted(range(2, n_orb, 2), key=lambda m: (m % 4 == 2, m))
    far = lax.ppermute(coefficients[0, :8], "orb", xor_pairs(n_orb, last))[:STEPS]

    def weights(columns, held):
        chosen = (owners[:, None] == jnp.stack([me ^ m for m in held])[None, :]).astype(f32)
        return jnp.sum(jnp.stack(columns)[:, :, None, :] * chosen[None, :, :, None], 1)

    def combined(columns, held, panels):
        return pl.pallas_call(
            functools.partial(combine_kernel, len(panels)),
            out_shape=(slab,) * len(columns),
            in_specs=[vmem] * (1 + len(panels)),
            out_specs=(vmem,) * len(columns),
        )(in_vmem(weights(columns, held)), *[in_vmem(p) for p in panels])

    panels = [panel] + [lax.ppermute(panel, "orb", xor_pairs(n_orb, m)) for m in near]
    beside = lax.ppermute(panel, "orb", xor_pairs(n_orb, 1))
    (sent,) = combined([far], [0, 1], [panel, beside])
    received = lax.ppermute(sent, "orb", xor_pairs(n_orb, last))
    mine, theirs = combined([coefficients[0, :STEPS], swapped[-1, :STEPS]], [0] + near, panels)
    rotated = mine + lax.ppermute(theirs, "orb", xor_pairs(n_orb, 1)) + received
    return tuple(jnp.transpose(x, (1, 0, 2))[None] for x in (panel, rotated))


def solution(mesh):
    placed = (
        P("orb", None, "dom", None),
        P(None, "dom", None),
        P("orb"),
        P(),
        P(None, None, "orb"),
    )
    return jax.shard_map(
        per_device,
        mesh=mesh,
        in_specs=placed,
        out_specs=(P("orb", None, "dom", None), P("orb", None, "dom", None)),
        check_vma=False,
    )
```

```python
import functools

import jax
import jax.numpy as jnp
import ml_dtypes
import numpy as np
from jax import lax
from jax.experimental import pallas as pl
from jax.experimental.pallas import tpu as pltpu
from jax.sharding import PartitionSpec as P

RADIUS = 6
MAXDEG = 8
STEPS = 4

STENCIL = (
    -5369.0 / 1800.0,
    12.0 / 7.0,
    -15.0 / 56.0,
    10.0 / 189.0,
    -1.0 / 112.0,
    2.0 / 1925.0,
    -1.0 / 16632.0,
)
FILTER_CENTER = 7.75
FILTER_HALF = 6.25
SCALE = 2.0 / FILTER_HALF
TAPS = tuple(-0.5 * SCALE * c for c in STENCIL[1:])
DIAGONAL = SCALE * (-1.5 * STENCIL[0] - FILTER_CENTER)


def xor_pairs(count, mask):
    return [(i, i ^ mask) for i in range(count)]


def shift_pairs(count, step):
    return [(i, i - step) for i in range(count) if 0 <= i - step < count]


def split(values):
    high = values.astype(jnp.bfloat16)
    return high, (values - high.astype(jnp.float32)).astype(jnp.bfloat16)


def stencil(count, cells):
    around = np.zeros((count, count), np.float64)
    for k, tap in enumerate(TAPS, 1):
        for i in range(count):
            around[i, (i + k) % count] += tap
            around[i, (i - k) % count] += tap
    between = sum(tap * (np.eye(cells, k=k) + np.eye(cells, k=-k)) for k, tap in enumerate(TAPS, 1))
    matrix = np.kron(np.eye(cells), around) + np.kron(between, np.eye(count))
    high = matrix.astype(ml_dtypes.bfloat16)
    low = (matrix - high.astype(np.float64)).astype(ml_dtypes.bfloat16)
    return high, low


class Layout:
    def __init__(self, n_dom, cells, planes, width):
        self.n_dom, self.cells, self.planes, self.width = n_dom, cells, planes, width
        halo = -(-RADIUS * MAXDEG // cells)
        self.whole = n_dom <= 2 * halo + 1
        if self.whole:
            self.slots = list(range(n_dom - 1, 0, -1))
            self.pairs = [xor_pairs(n_dom, k) for k in self.slots]
            self.window = n_dom * cells
            extents = {min(cells + 2 * RADIUS * left, self.window) for left in range(MAXDEG)}
        else:
            self.slots = [s * k for k in range(1, halo + 1) for s in (1, -1)]
            self.pairs = [shift_pairs(n_dom, k) for k in self.slots]
            self.window = (2 * halo + 1) * cells
            extents = {cells}
        self.groups = sorted({max(g for g in range(1, width // planes + 1) if e % (2 * g) == 0) for e in extents})
        high, low = stencil(width, 1)
        across = np.block([[high, low], [high, low]])
        self.matrices = [across] + [np.block([[m, m] for m in stencil(planes, g)]) for g in self.groups]

    def home(self):
        return lax.axis_index("dom") if self.whole else self.window // self.cells // 2

    def starts(self):
        home = self.home()
        return [(home ^ k if self.whole else home + k) * self.cells for k in [0] + self.slots]

    def on_grid(self, reach, act):
        home, dom = self.home(), lax.axis_index("dom")
        for block in range(home - reach, home + reach + 1):
            place = dom + block - home
            pl.when((place >= 0) & (place < self.n_dom))(functools.partial(act, block))


def apply_taps(layout, matrices, source, target, shift, base, extent, begin):
    planes, width = layout.planes, layout.width
    high, low = split(source[pl.ds(RADIUS + base, extent)].reshape(extent * planes, width))
    across = jnp.dot(jnp.concatenate([high, low], 1), matrices[0][...], preferred_element_type=jnp.float32)
    group = max(m for m in layout.groups if extent % (2 * m) == 0)
    size = group * planes
    alongs = []
    for top in range(0, extent * planes, 2 * size):
        pieces = [jnp.concatenate([v[top : top + size], v[top + size : top + 2 * size]], 1) for v in (high, low)]
        matrix = matrices[1 + layout.groups.index(group)]
        alongs.append(jnp.dot(matrix[...], jnp.concatenate(pieces, 0), preferred_element_type=jnp.float32))
    for tile in range(0, extent, group):
        x = RADIUS + base + tile
        below = [source[x - RADIUS + j] for j in range(RADIUS)]
        above = [source[x + group + j] for j in range(RADIUS)]
        for i in range(group):
            terms = begin(base + tile + i)
            for k in range(1, RADIUS + 1):
                outside = ([below[RADIUS + i - k]] if i < k else []) + ([above[i + k - group]] if i + k >= group else [])
                if outside:
                    terms.append(TAPS[k - 1] * functools.reduce(jnp.add, outside))
            target[shift + base + tile + i] = functools.reduce(jnp.add, terms)
    for index, along in enumerate(alongs):
        along = along[:size] + along[size:]
        for half in range(2):
            top = (2 * index + half) * size
            plane_sum = across[top : top + size, :width] + across[top : top + size, width:]
            plane_sum = plane_sum + along[:, half * width : (half + 1) * width]
            spot = pl.ds(shift + base + (2 * index + half) * group, group)
            target[spot] = target[spot] + plane_sum.reshape(group, planes, width)


def early_kernel(*refs):
    count = len(refs) // 2
    refs[count][0] = refs[0][0]
    for source, target in zip(refs[1:count], refs[count + 1 :]):
        target[...] = source[...]


def halves_kernel(cells, coefficients_ref, *refs):
    *blocks, out_ref = refs
    half = cells // 2
    for index, block in enumerate(blocks):
        out_ref[pl.ds(index * half, half)] = block[cells:]
    out_ref[pl.ds(len(blocks) * half, 1)] = coefficients_ref[...]


def open_kernel(layout, *refs):
    count = len(layout.matrices)
    matrices, blocks, (start_ref, taps_ref) = refs[:count], refs[count:-2], refs[-2:]
    cells, window = layout.cells, layout.window
    edge = jnp.zeros((RADIUS, layout.planes, layout.width), jnp.float32)
    start_ref[pl.ds(0, RADIUS)] = edge
    start_ref[pl.ds(RADIUS + window, RADIUS)] = edge
    for start, block in zip(layout.starts(), blocks):
        start_ref[pl.ds(RADIUS + start, cells)] = block[:cells]

    def act(base, extent):
        apply_taps(layout, matrices, start_ref, taps_ref, 0, base, extent, lambda x: [])

    if layout.whole:
        act(0, window)
    else:
        taps_ref[...] = jnp.zeros(taps_ref.shape, jnp.float32)
        layout.on_grid(window // cells // 2, lambda block: act(block * cells, cells))


def chain_kernel(layout, degree_ref, *refs):
    count = len(layout.matrices)
    matrices, (own_ref, swapped_ref, start_ref, taps_ref), refs = refs[:count], refs[count : count + 4], refs[count + 4 :]
    blocks, (out_ref, *fields, potential) = refs[: len(layout.slots)], refs[len(layout.slots) :]
    cells, window = layout.cells, layout.window
    half = cells // 2
    core = lax.axis_index("orb") % 2
    degree = degree_ref[0]
    home = layout.home()

    starts = layout.starts()
    potential[pl.ds(starts[0], cells)] = SCALE * own_ref[...] + DIAGONAL
    for index, (start, block) in enumerate(zip(starts[1:], blocks)):
        potential[pl.ds(start + core * half, half)] = SCALE * block[cells:] + DIAGONAL
        other = swapped_ref[index * half : (index + 1) * half]
        potential[pl.ds(start + (1 - core) * half, half)] = SCALE * other + DIAGONAL

    def begin(current, previous):
        previous[...] = start_ref[...]
        current[pl.ds(0, RADIUS)] = start_ref[pl.ds(0, RADIUS)]
        current[pl.ds(RADIUS + window, RADIUS)] = start_ref[pl.ds(RADIUS + window, RADIUS)]
        for x in range(0, window, RADIUS):
            here = pl.ds(RADIUS + x, RADIUS)
            current[here] = 0.5 * (taps_ref[pl.ds(x, RADIUS)] + potential[pl.ds(x, RADIUS)] * start_ref[here])

    pl.when(degree % 2 == 1)(functools.partial(begin, fields[0], fields[1]))
    pl.when(degree % 2 == 0)(functools.partial(begin, fields[1], fields[0]))

    def level(parity, reach):
        source, target = fields[1 - parity], fields[parity]

        def act(base, extent):
            def first(x):
                return [potential[x] * source[RADIUS + x] - target[RADIUS + x]]

            apply_taps(layout, matrices, source, target, RADIUS, base, extent, first)

        if layout.whole:
            extent = min(cells + 2 * reach, window)
            act(jnp.clip(home * cells - reach, 0, window - extent), extent)
        else:
            layout.on_grid(-(-reach // cells), lambda block: act(block * cells, cells))

    def levels(fewest, most, reach):
        parity = fewest % 2
        total = jnp.maximum(jnp.minimum(most, degree - 2) - fewest + 1, 0)

        def pair(index, carry):
            level(1 - parity, reach)
            level(parity, reach)
            return carry

        pl.when(total % 2 == 1)(lambda: level(parity, reach))
        if most > fewest:
            lax.fori_loop(0, total // 2, pair, 0)

    bounds = [RADIUS * left for left in range(MAXDEG - 1)]
    if layout.whole:
        bounds = [min(reach, (window - cells + 1) // 2) for reach in bounds]
    for reach in sorted(set(bounds), reverse=True):
        lefts = [left for left in range(MAXDEG - 1) if bounds[left] == reach]
        levels(lefts[0], lefts[-1], reach)
    out_ref[...] = fields[0][pl.ds(RADIUS + home * cells, cells)]


def combine_kernel(count, weights_ref, *refs):
    panels, outs = refs[:count], refs[count:]
    for out, ref in enumerate(outs):
        total = None
        for index, panel in enumerate(panels):
            term = weights_ref[out, index : index + 1] * panel[...]
            total = term if total is None else total + term
        ref[...] = total


def in_vmem(x):
    return pltpu.with_memory_space_constraint(x, pltpu.VMEM)


def per_device(orbitals, potential, degree, owners, rotation):
    _, planes, cells, width = orbitals.shape
    n_orb = lax.axis_size("orb")
    me = lax.axis_index("orb")
    layout = Layout(lax.axis_size("dom"), cells, planes, width)
    vmem = pl.BlockSpec(memory_space=pltpu.VMEM)
    smem = pl.BlockSpec(memory_space=pltpu.SMEM)
    f32 = jnp.float32
    slab = pltpu.VMEM((cells, planes, width), f32)
    window = pltpu.VMEM((layout.window, planes, width), f32)
    padded = pltpu.VMEM((layout.window + 2 * RADIUS, planes, width), f32)

    orbital = jnp.transpose(orbitals[0], (1, 0, 2)).astype(f32)
    potential = jnp.transpose(potential, (1, 0, 2))
    half = lax.dynamic_slice_in_dim(potential, me % 2 * (cells // 2), cells // 2, 0)
    packed = jnp.concatenate([orbital, half], 0)
    arrived = [lax.ppermute(packed, "dom", p) for p in layout.pairs]
    matrices = [in_vmem(jnp.asarray(m)) for m in layout.matrices]
    column = rotation[:, 0, 0].astype(f32)
    early = pl.pallas_call(
        early_kernel,
        out_shape=[pltpu.SMEM((1,), jnp.int32)] + [pltpu.VMEM(m.shape, m.dtype) for m in layout.matrices],
        in_specs=[smem] + [vmem] * len(matrices),
        out_specs=[smem] + [vmem] * len(matrices),
    )(degree, *matrices)
    column, degree, *matrices = lax.optimization_barrier((column, *early))
    matrices = [in_vmem(m) for m in matrices]
    coefficients = jnp.pad(column, (0, planes - STEPS))
    coefficients = jnp.broadcast_to(coefficients[None, :, None], (1, planes, width))
    halves = pl.pallas_call(
        functools.partial(halves_kernel, cells),
        out_shape=pltpu.VMEM((len(arrived) * (cells // 2) + 1, planes, width), f32),
        in_specs=[vmem] * (1 + len(arrived)),
        out_specs=vmem,
    )(*[in_vmem(x) for x in [coefficients] + arrived])
    swapped = lax.ppermute(halves, "orb", xor_pairs(n_orb, 1))

    operands = matrices + [in_vmem(x) for x in [packed] + arrived]
    start, taps = pl.pallas_call(
        functools.partial(open_kernel, layout),
        out_shape=(padded, window),
        in_specs=[vmem] * len(operands),
        out_specs=(vmem, vmem),
    )(*operands)
    operands = matrices + [in_vmem(x) for x in [potential, swapped, start, taps] + arrived]
    panel = pl.pallas_call(
        functools.partial(chain_kernel, layout),
        out_shape=slab,
        in_specs=[smem] + [vmem] * len(operands),
        out_specs=vmem,
        scratch_shapes=[padded, padded, window],
    )(pltpu.with_memory_space_constraint(degree, pltpu.SMEM), *operands)

    *near, last = sorted(range(2, n_orb, 2), key=lambda m: (m % 4 == 2, m))
    far = lax.ppermute(coefficients[0, :8], "orb", xor_pairs(n_orb, last))[:STEPS]

    def weights(columns, held):
        chosen = (owners[:, None] == jnp.stack([me ^ m for m in held])[None, :]).astype(f32)
        return jnp.sum(jnp.stack(columns)[:, :, None, :] * chosen[None, :, :, None], 1)

    def combined(columns, held, panels):
        return pl.pallas_call(
            functools.partial(combine_kernel, len(panels)),
            out_shape=(slab,) * len(columns),
            in_specs=[vmem] * (1 + len(panels)),
            out_specs=(vmem,) * len(columns),
        )(in_vmem(weights(columns, held)), *[in_vmem(p) for p in panels])

    panels = [panel] + [lax.ppermute(panel, "orb", xor_pairs(n_orb, m)) for m in near]
    beside = lax.ppermute(panel, "orb", xor_pairs(n_orb, 1))
    (sent,) = combined([far], [0, 1], [panel, beside])
    received = lax.ppermute(sent, "orb", xor_pairs(n_orb, last))
    mine, theirs = combined([coefficients[0, :STEPS], swapped[-1, :STEPS]], [0] + near, panels)
    rotated = mine + lax.ppermute(theirs, "orb", xor_pairs(n_orb, 1)) + received
    return tuple(jnp.transpose(x, (1, 0, 2))[None] for x in (panel, rotated))


def solution(mesh):
    placed = (
        P("orb", None, "dom", None),
        P(None, "dom", None),
        P("orb"),
        P(),
        P(None, None, "orb"),
    )
    return jax.shard_map(
        per_device,
        mesh=mesh,
        in_specs=placed,
        out_specs=(P("orb", None, "dom", None), P("orb", None, "dom", None)),
        check_vma=False,
    )
```

```python
import functools

import jax
import jax.numpy as jnp
import ml_dtypes
import numpy as np
from jax import lax
from jax.experimental import pallas as pl
from jax.experimental.pallas import tpu as pltpu
from jax.sharding import PartitionSpec as P

RADIUS = 6
MAXDEG = 8
STEPS = 4

STENCIL = (
    -5369.0 / 1800.0,
    12.0 / 7.0,
    -15.0 / 56.0,
    10.0 / 189.0,
    -1.0 / 112.0,
    2.0 / 1925.0,
    -1.0 / 16632.0,
)
FILTER_CENTER = 7.75
FILTER_HALF = 6.25
SCALE = 2.0 / FILTER_HALF
TAPS = tuple(-0.5 * SCALE * c for c in STENCIL[1:])
DIAGONAL = SCALE * (-1.5 * STENCIL[0] - FILTER_CENTER)


def xor_pairs(count, mask):
    return [(i, i ^ mask) for i in range(count)]


def shift_pairs(count, step):
    return [(i, i - step) for i in range(count) if 0 <= i - step < count]


def split(values):
    high = values.astype(jnp.bfloat16)
    return high, (values - high.astype(jnp.float32)).astype(jnp.bfloat16)


def stencil(count, cells):
    around = np.zeros((count, count), np.float64)
    for k, tap in enumerate(TAPS, 1):
        for i in range(count):
            around[i, (i + k) % count] += tap
            around[i, (i - k) % count] += tap
    between = sum(tap * (np.eye(cells, k=k) + np.eye(cells, k=-k)) for k, tap in enumerate(TAPS, 1))
    matrix = np.kron(np.eye(cells), around) + np.kron(between, np.eye(count))
    high = matrix.astype(ml_dtypes.bfloat16)
    low = (matrix - high.astype(np.float64)).astype(ml_dtypes.bfloat16)
    return high, low


class Layout:
    def __init__(self, n_dom, cells, planes, width):
        self.n_dom, self.cells, self.planes, self.width = n_dom, cells, planes, width
        halo = -(-RADIUS * MAXDEG // cells)
        self.whole = n_dom <= 2 * halo + 1
        if self.whole:
            self.slots = list(range(n_dom - 1, 0, -1))
            self.pairs = [xor_pairs(n_dom, k) for k in self.slots]
            self.window = n_dom * cells
            extents = {min(cells + 2 * RADIUS * left, self.window) for left in range(MAXDEG)}
        else:
            self.slots = [s * k for k in range(1, halo + 1) for s in (1, -1)]
            self.pairs = [shift_pairs(n_dom, k) for k in self.slots]
            self.window = (2 * halo + 1) * cells
            extents = {cells}
        self.groups = sorted({max(g for g in range(1, width // planes + 1) if e % (2 * g) == 0) for e in extents})
        high, low = stencil(width, 1)
        across = np.block([[high, low], [high, low]])
        self.matrices = [across] + [np.block([[m, m] for m in stencil(planes, g)]) for g in self.groups]

    def home(self):
        return lax.axis_index("dom") if self.whole else self.window // self.cells // 2

    def starts(self):
        home = self.home()
        return [(home ^ k if self.whole else home + k) * self.cells for k in [0] + self.slots]

    def on_grid(self, reach, act):
        home, dom = self.home(), lax.axis_index("dom")
        for block in range(home - reach, home + reach + 1):
            place = dom + block - home
            pl.when((place >= 0) & (place < self.n_dom))(functools.partial(act, block))


def apply_taps(layout, matrices, source, target, shift, base, extent, begin):
    planes, width = layout.planes, layout.width
    high, low = split(source[pl.ds(RADIUS + base, extent)].reshape(extent * planes, width))
    across = jnp.dot(jnp.concatenate([high, low], 1), matrices[0][...], preferred_element_type=jnp.float32)
    group = max(m for m in layout.groups if extent % (2 * m) == 0)
    size = group * planes
    alongs = []
    for top in range(0, extent * planes, 2 * size):
        pieces = [jnp.concatenate([v[top : top + size], v[top + size : top + 2 * size]], 1) for v in (high, low)]
        matrix = matrices[1 + layout.groups.index(group)]
        alongs.append(jnp.dot(matrix[...], jnp.concatenate(pieces, 0), preferred_element_type=jnp.float32))
    for tile in range(0, extent, group):
        x = RADIUS + base + tile
        below = [source[x - RADIUS + j] for j in range(RADIUS)]
        above = [source[x + group + j] for j in range(RADIUS)]
        for i in range(group):
            terms = begin(base + tile + i)
            for k in range(1, RADIUS + 1):
                outside = ([below[RADIUS + i - k]] if i < k else []) + ([above[i + k - group]] if i + k >= group else [])
                if outside:
                    terms.append(TAPS[k - 1] * functools.reduce(jnp.add, outside))
            target[shift + base + tile + i] = functools.reduce(jnp.add, terms)
    for index, along in enumerate(alongs):
        along = along[:size] + along[size:]
        for half in range(2):
            top = (2 * index + half) * size
            plane_sum = across[top : top + size, :width] + across[top : top + size, width:]
            plane_sum = plane_sum + along[:, half * width : (half + 1) * width]
            spot = pl.ds(shift + base + (2 * index + half) * group, group)
            target[spot] = target[spot] + plane_sum.reshape(group, planes, width)


def early_kernel(*refs):
    count = len(refs) // 2
    refs[count][0] = refs[0][0]
    for source, target in zip(refs[1:count], refs[count + 1 :]):
        target[...] = source[...]


def halves_kernel(cells, coefficients_ref, *refs):
    *blocks, out_ref = refs
    half = cells // 2
    for index, block in enumerate(blocks):
        out_ref[pl.ds(index * half, half)] = block[cells:]
    out_ref[pl.ds(len(blocks) * half, 1)] = coefficients_ref[...]


def open_kernel(layout, *refs):
    count = len(layout.matrices)
    matrices, blocks, (start_ref, taps_ref) = refs[:count], refs[count:-2], refs[-2:]
    cells, window = layout.cells, layout.window
    edge = jnp.zeros((RADIUS, layout.planes, layout.width), jnp.float32)
    start_ref[pl.ds(0, RADIUS)] = edge
    start_ref[pl.ds(RADIUS + window, RADIUS)] = edge
    for start, block in zip(layout.starts(), blocks):
        start_ref[pl.ds(RADIUS + start, cells)] = block[:cells]

    def act(base, extent):
        apply_taps(layout, matrices, start_ref, taps_ref, 0, base, extent, lambda x: [])

    if layout.whole:
        act(0, window)
    else:
        taps_ref[...] = jnp.zeros(taps_ref.shape, jnp.float32)
        layout.on_grid(window // cells // 2, lambda block: act(block * cells, cells))


def chain_kernel(layout, degree_ref, *refs):
    count = len(layout.matrices)
    matrices, (own_ref, swapped_ref, start_ref, taps_ref), refs = refs[:count], refs[count : count + 4], refs[count + 4 :]
    blocks, (out_ref, *fields, potential) = refs[: len(layout.slots)], refs[len(layout.slots) :]
    cells, window = layout.cells, layout.window
    half = cells // 2
    core = lax.axis_index("orb") % 2
    degree = degree_ref[0]
    home = layout.home()

    starts = layout.starts()
    potential[pl.ds(starts[0], cells)] = SCALE * own_ref[...] + DIAGONAL
    for index, (start, block) in enumerate(zip(starts[1:], blocks)):
        potential[pl.ds(start + core * half, half)] = SCALE * block[cells:] + DIAGONAL
        other = swapped_ref[index * half : (index + 1) * half]
        potential[pl.ds(start + (1 - core) * half, half)] = SCALE * other + DIAGONAL

    def begin(current, previous):
        for x in range(-RADIUS, window + RADIUS, RADIUS):
            here = pl.ds(RADIUS + x, RADIUS)
            given = start_ref[here]
            previous[here] = given
            if 0 <= x < window:
                given = 0.5 * (taps_ref[pl.ds(x, RADIUS)] + potential[pl.ds(x, RADIUS)] * given)
            current[here] = given

    pl.when(degree % 2 == 1)(functools.partial(begin, fields[0], fields[1]))
    pl.when(degree % 2 == 0)(functools.partial(begin, fields[1], fields[0]))

    def level(parity, reach):
        source, target = fields[1 - parity], fields[parity]

        def act(base, extent):
            def first(x):
                return [potential[x] * source[RADIUS + x] - target[RADIUS + x]]

            apply_taps(layout, matrices, source, target, RADIUS, base, extent, first)

        if layout.whole:
            extent = min(cells + 2 * reach, window)
            act(jnp.clip(home * cells - reach, 0, window - extent), extent)
        else:
            layout.on_grid(-(-reach // cells), lambda block: act(block * cells, cells))

    def levels(fewest, most, reach):
        parity = fewest % 2
        total = jnp.maximum(jnp.minimum(most, degree - 2) - fewest + 1, 0)

        def pair(index, carry):
            level(1 - parity, reach)
            level(parity, reach)
            return carry

        pl.when(total % 2 == 1)(lambda: level(parity, reach))
        if most > fewest:
            lax.fori_loop(0, total // 2, pair, 0)

    bounds = [RADIUS * left for left in range(MAXDEG - 1)]
    if layout.whole:
        bounds = [min(reach, (window - cells + 1) // 2) for reach in bounds]
    for reach in sorted(set(bounds), reverse=True):
        lefts = [left for left in range(MAXDEG - 1) if bounds[left] == reach]
        levels(lefts[0], lefts[-1], reach)
    out_ref[...] = fields[0][pl.ds(RADIUS + home * cells, cells)]


def combine_kernel(count, weights_ref, *refs):
    panels, outs = refs[:count], refs[count:]
    for out, ref in enumerate(outs):
        total = None
        for index, panel in enumerate(panels):
            term = weights_ref[out, index : index + 1] * panel[...]
            total = term if total is None else total + term
        ref[...] = total


def in_vmem(x):
    return pltpu.with_memory_space_constraint(x, pltpu.VMEM)


def per_device(orbitals, potential, degree, owners, rotation):
    _, planes, cells, width = orbitals.shape
    n_orb = lax.axis_size("orb")
    me = lax.axis_index("orb")
    layout = Layout(lax.axis_size("dom"), cells, planes, width)
    vmem = pl.BlockSpec(memory_space=pltpu.VMEM)
    smem = pl.BlockSpec(memory_space=pltpu.SMEM)
    f32 = jnp.float32
    slab = pltpu.VMEM((cells, planes, width), f32)
    window = pltpu.VMEM((layout.window, planes, width), f32)
    padded = pltpu.VMEM((layout.window + 2 * RADIUS, planes, width), f32)

    orbital = jnp.transpose(orbitals[0], (1, 0, 2)).astype(f32)
    potential = jnp.transpose(potential, (1, 0, 2))
    half = lax.dynamic_slice_in_dim(potential, me % 2 * (cells // 2), cells // 2, 0)
    packed = jnp.concatenate([orbital, half], 0)
    arrived = [lax.ppermute(packed, "dom", p) for p in layout.pairs]
    matrices = [in_vmem(jnp.asarray(m)) for m in layout.matrices]
    column = rotation[:, 0, 0].astype(f32)
    early = pl.pallas_call(
        early_kernel,
        out_shape=[pltpu.SMEM((1,), jnp.int32)] + [pltpu.VMEM(m.shape, m.dtype) for m in layout.matrices],
        in_specs=[smem] + [vmem] * len(matrices),
        out_specs=[smem] + [vmem] * len(matrices),
    )(degree, *matrices)
    column, degree, *matrices = lax.optimization_barrier((column, *early))
    matrices = [in_vmem(m) for m in matrices]
    coefficients = jnp.pad(column, (0, planes - STEPS))
    coefficients = jnp.broadcast_to(coefficients[None, :, None], (1, planes, width))
    halves = pl.pallas_call(
        functools.partial(halves_kernel, cells),
        out_shape=pltpu.VMEM((len(arrived) * (cells // 2) + 1, planes, width), f32),
        in_specs=[vmem] * (1 + len(arrived)),
        out_specs=vmem,
    )(*[in_vmem(x) for x in [coefficients] + arrived])
    swapped = lax.ppermute(halves, "orb", xor_pairs(n_orb, 1))

    operands = matrices + [in_vmem(x) for x in [packed] + arrived]
    start, taps = pl.pallas_call(
        functools.partial(open_kernel, layout),
        out_shape=(padded, window),
        in_specs=[vmem] * len(operands),
        out_specs=(vmem, vmem),
    )(*operands)
    operands = matrices + [in_vmem(x) for x in [potential, swapped, start, taps] + arrived]
    panel = pl.pallas_call(
        functools.partial(chain_kernel, layout),
        out_shape=slab,
        in_specs=[smem] + [vmem] * len(operands),
        out_specs=vmem,
        scratch_shapes=[padded, padded, window],
    )(pltpu.with_memory_space_constraint(degree, pltpu.SMEM), *operands)

    *near, last = sorted(range(2, n_orb, 2), key=lambda m: (m % 4 == 2, m))
    far = lax.ppermute(coefficients[0, :8], "orb", xor_pairs(n_orb, last))[:STEPS]

    def weights(columns, held):
        chosen = (owners[:, None] == jnp.stack([me ^ m for m in held])[None, :]).astype(f32)
        return jnp.sum(jnp.stack(columns)[:, :, None, :] * chosen[None, :, :, None], 1)

    def combined(columns, held, panels):
        return pl.pallas_call(
            functools.partial(combine_kernel, len(panels)),
            out_shape=(slab,) * len(columns),
            in_specs=[vmem] * (1 + len(panels)),
            out_specs=(vmem,) * len(columns),
        )(in_vmem(weights(columns, held)), *[in_vmem(p) for p in panels])

    panels = [panel] + [lax.ppermute(panel, "orb", xor_pairs(n_orb, m)) for m in near]
    beside = lax.ppermute(panel, "orb", xor_pairs(n_orb, 1))
    (sent,) = combined([far], [0, 1], [panel, beside])
    received = lax.ppermute(sent, "orb", xor_pairs(n_orb, last))
    mine, theirs = combined([coefficients[0, :STEPS], swapped[-1, :STEPS]], [0] + near, panels)
    rotated = mine + lax.ppermute(theirs, "orb", xor_pairs(n_orb, 1)) + received
    return tuple(jnp.transpose(x, (1, 0, 2))[None] for x in (panel, rotated))


def solution(mesh):
    placed = (
        P("orb", None, "dom", None),
        P(None, "dom", None),
        P("orb"),
        P(),
        P(None, None, "orb"),
    )
    return jax.shard_map(
        per_device,
        mesh=mesh,
        in_specs=placed,
        out_specs=(P("orb", None, "dom", None), P("orb", None, "dom", None)),
        check_vma=False,
    )
```

```python
import functools

import jax
import jax.numpy as jnp
import ml_dtypes
import numpy as np
from jax import lax
from jax.experimental import pallas as pl
from jax.experimental.pallas import tpu as pltpu
from jax.sharding import PartitionSpec as P

RADIUS = 6
MAXDEG = 8
STEPS = 4

STENCIL = (
    -5369.0 / 1800.0,
    12.0 / 7.0,
    -15.0 / 56.0,
    10.0 / 189.0,
    -1.0 / 112.0,
    2.0 / 1925.0,
    -1.0 / 16632.0,
)
FILTER_CENTER = 7.75
FILTER_HALF = 6.25
SCALE = 2.0 / FILTER_HALF
TAPS = tuple(-0.5 * SCALE * c for c in STENCIL[1:])
DIAGONAL = SCALE * (-1.5 * STENCIL[0] - FILTER_CENTER)


def xor_pairs(count, mask):
    return [(i, i ^ mask) for i in range(count)]


def shift_pairs(count, step):
    return [(i, i - step) for i in range(count) if 0 <= i - step < count]


def split(values):
    high = values.astype(jnp.bfloat16)
    return high, (values - high.astype(jnp.float32)).astype(jnp.bfloat16)


def stencil(count, cells):
    around = np.zeros((count, count), np.float64)
    for k, tap in enumerate(TAPS, 1):
        for i in range(count):
            around[i, (i + k) % count] += tap
            around[i, (i - k) % count] += tap
    between = sum(tap * (np.eye(cells, k=k) + np.eye(cells, k=-k)) for k, tap in enumerate(TAPS, 1))
    matrix = np.kron(np.eye(cells), around) + np.kron(between, np.eye(count))
    high = matrix.astype(ml_dtypes.bfloat16)
    low = (matrix - high.astype(np.float64)).astype(ml_dtypes.bfloat16)
    return high, low


class Layout:
    def __init__(self, n_dom, cells, planes, width):
        self.n_dom, self.cells, self.planes, self.width = n_dom, cells, planes, width
        halo = -(-RADIUS * MAXDEG // cells)
        self.whole = n_dom <= 2 * halo + 1
        if self.whole:
            self.slots = list(range(n_dom - 1, 0, -1))
            self.pairs = [xor_pairs(n_dom, k) for k in self.slots]
            self.window = n_dom * cells
            extents = {min(cells + 2 * RADIUS * left, self.window) for left in range(MAXDEG)}
        else:
            self.slots = [s * k for k in range(1, halo + 1) for s in (1, -1)]
            self.pairs = [shift_pairs(n_dom, k) for k in self.slots]
            self.window = (2 * halo + 1) * cells
            extents = {cells}
        self.groups = sorted({max(g for g in range(1, width // planes + 1) if e % (2 * g) == 0) for e in extents})
        high, low = stencil(width, 1)
        across = np.block([[high, low], [high, low]])
        self.matrices = [across] + [np.block([[m, m] for m in stencil(planes, g)]) for g in self.groups]

    def home(self):
        return lax.axis_index("dom") if self.whole else self.window // self.cells // 2

    def starts(self):
        home = self.home()
        return [(home ^ k if self.whole else home + k) * self.cells for k in [0] + self.slots]

    def on_grid(self, reach, act):
        home, dom = self.home(), lax.axis_index("dom")
        for block in range(home - reach, home + reach + 1):
            place = dom + block - home
            pl.when((place >= 0) & (place < self.n_dom))(functools.partial(act, block))


def apply_taps(layout, matrices, source, target, shift, base, extent, begin):
    planes, width = layout.planes, layout.width
    high, low = split(source[pl.ds(RADIUS + base, extent)].reshape(extent * planes, width))
    across = jnp.dot(jnp.concatenate([high, low], 1), matrices[0][...], preferred_element_type=jnp.float32)
    group = max(m for m in layout.groups if extent % (2 * m) == 0)
    size = group * planes
    alongs = []
    for top in range(0, extent * planes, 2 * size):
        pieces = [jnp.concatenate([v[top : top + size], v[top + size : top + 2 * size]], 1) for v in (high, low)]
        matrix = matrices[1 + layout.groups.index(group)]
        alongs.append(jnp.dot(matrix[...], jnp.concatenate(pieces, 0), preferred_element_type=jnp.float32))
    for tile in range(0, extent, group):
        x = RADIUS + base + tile
        below = [source[x - RADIUS + j] for j in range(RADIUS)]
        above = [source[x + group + j] for j in range(RADIUS)]
        for i in range(group):
            terms = begin(base + tile + i)
            for k in range(1, RADIUS + 1):
                outside = ([below[RADIUS + i - k]] if i < k else []) + ([above[i + k - group]] if i + k >= group else [])
                if outside:
                    terms.append(TAPS[k - 1] * functools.reduce(jnp.add, outside))
            target[shift + base + tile + i] = functools.reduce(jnp.add, terms)
    for index, along in enumerate(alongs):
        along = along[:size] + along[size:]
        for half in range(2):
            top = (2 * index + half) * size
            plane_sum = across[top : top + size, :width] + across[top : top + size, width:]
            plane_sum = plane_sum + along[:, half * width : (half + 1) * width]
            spot = pl.ds(shift + base + (2 * index + half) * group, group)
            target[spot] = target[spot] + plane_sum.reshape(group, planes, width)


def early_kernel(*refs):
    count = len(refs) // 2
    refs[count][0] = refs[0][0]
    for source, target in zip(refs[1:count], refs[count + 1 :]):
        target[...] = source[...]


def halves_kernel(cells, coefficients_ref, *refs):
    *blocks, out_ref = refs
    half = cells // 2
    for index, block in enumerate(blocks):
        out_ref[pl.ds(index * half, half)] = block[cells:]
    out_ref[pl.ds(len(blocks) * half, 1)] = coefficients_ref[...]


def open_kernel(layout, *refs):
    count = len(layout.matrices)
    matrices, blocks, (start_ref, taps_ref) = refs[:count], refs[count:-2], refs[-2:]
    cells, window = layout.cells, layout.window
    edge = jnp.zeros((RADIUS, layout.planes, layout.width), jnp.float32)
    start_ref[pl.ds(0, RADIUS)] = edge
    start_ref[pl.ds(RADIUS + window, RADIUS)] = edge
    for start, block in zip(layout.starts(), blocks):
        start_ref[pl.ds(RADIUS + start, cells)] = block[:cells]

    def act(base, extent):
        apply_taps(layout, matrices, start_ref, taps_ref, 0, base, extent, lambda x: [])

    if layout.whole:
        act(0, window)
    else:
        taps_ref[...] = jnp.zeros(taps_ref.shape, jnp.float32)
        layout.on_grid(window // cells // 2, lambda block: act(block * cells, cells))


def chain_kernel(layout, degree_ref, *refs):
    count = len(layout.matrices)
    matrices, (own_ref, swapped_ref, start_ref, taps_ref), refs = refs[:count], refs[count : count + 4], refs[count + 4 :]
    blocks, (out_ref, *fields, potential) = refs[: len(layout.slots)], refs[len(layout.slots) :]
    cells, window = layout.cells, layout.window
    half = cells // 2
    core = lax.axis_index("orb") % 2
    degree = degree_ref[0]
    home = layout.home()

    starts = layout.starts()
    potential[pl.ds(starts[0], cells)] = SCALE * own_ref[...] + DIAGONAL
    for index, (start, block) in enumerate(zip(starts[1:], blocks)):
        potential[pl.ds(start + core * half, half)] = SCALE * block[cells:] + DIAGONAL
        other = swapped_ref[index * half : (index + 1) * half]
        potential[pl.ds(start + (1 - core) * half, half)] = SCALE * other + DIAGONAL

    def begin(current, previous):
        for x in range(-RADIUS, window + RADIUS, RADIUS):
            here = pl.ds(RADIUS + x, RADIUS)
            given = start_ref[here]
            previous[here] = given
            if 0 <= x < window:
                given = 0.5 * (taps_ref[pl.ds(x, RADIUS)] + potential[pl.ds(x, RADIUS)] * given)
            current[here] = given

    pl.when(degree % 2 == 1)(functools.partial(begin, fields[0], fields[1]))
    pl.when(degree % 2 == 0)(functools.partial(begin, fields[1], fields[0]))

    def level(parity, reach):
        source, target = fields[1 - parity], fields[parity]

        def act(base, extent):
            def first(x):
                return [potential[x] * source[RADIUS + x] - target[RADIUS + x]]

            apply_taps(layout, matrices, source, target, RADIUS, base, extent, first)

        if layout.whole:
            extent = min(cells + 2 * reach, window)
            act(jnp.clip(home * cells - reach, 0, window - extent), extent)
        else:
            layout.on_grid(-(-reach // cells), lambda block: act(block * cells, cells))

    def levels(fewest, most, reach):
        parity = fewest % 2
        total = jnp.maximum(jnp.minimum(most, degree - 2) - fewest + 1, 0)

        def pair(index, carry):
            level(1 - parity, reach)
            level(parity, reach)
            return carry

        pl.when(total % 2 == 1)(lambda: level(parity, reach))
        if most > fewest:
            lax.fori_loop(0, total // 2, pair, 0)

    bounds = [RADIUS * left for left in range(MAXDEG - 1)]
    if layout.whole:
        bounds = [min(reach, (window - cells + 1) // 2) for reach in bounds]
    for reach in sorted(set(bounds), reverse=True):
        lefts = [left for left in range(MAXDEG - 1) if bounds[left] == reach]
        levels(lefts[0], lefts[-1], reach)
    out_ref[...] = fields[0][pl.ds(RADIUS + home * cells, cells)]


def combine_kernel(count, weights_ref, *refs):
    panels, outs = refs[:count], refs[count:]
    for out, ref in enumerate(outs):
        total = None
        for index, panel in enumerate(panels):
            term = weights_ref[out, index : index + 1] * panel[...]
            total = term if total is None else total + term
        ref[...] = total


def in_vmem(x):
    return pltpu.with_memory_space_constraint(x, pltpu.VMEM)


def per_device(orbitals, potential, degree, owners, rotation):
    _, planes, cells, width = orbitals.shape
    n_orb = lax.axis_size("orb")
    me = lax.axis_index("orb")
    layout = Layout(lax.axis_size("dom"), cells, planes, width)
    vmem = pl.BlockSpec(memory_space=pltpu.VMEM)
    smem = pl.BlockSpec(memory_space=pltpu.SMEM)
    f32 = jnp.float32
    slab = pltpu.VMEM((cells, planes, width), f32)
    window = pltpu.VMEM((layout.window, planes, width), f32)
    padded = pltpu.VMEM((layout.window + 2 * RADIUS, planes, width), f32)

    orbital = jnp.transpose(orbitals[0], (1, 0, 2)).astype(f32)
    potential = jnp.transpose(potential, (1, 0, 2))
    half = lax.dynamic_slice_in_dim(potential, me % 2 * (cells // 2), cells // 2, 0)
    packed = jnp.concatenate([orbital, half], 0)
    arrived = [lax.ppermute(packed, "dom", p) for p in layout.pairs]
    matrices = [in_vmem(jnp.asarray(m)) for m in layout.matrices]
    column = rotation[:, 0, 0].astype(f32)
    early = pl.pallas_call(
        early_kernel,
        out_shape=[pltpu.SMEM((1,), jnp.int32)] + [pltpu.VMEM(m.shape, m.dtype) for m in layout.matrices],
        in_specs=[smem] + [vmem] * len(matrices),
        out_specs=[smem] + [vmem] * len(matrices),
    )(degree, *matrices)
    column, degree, *matrices = lax.optimization_barrier((column, *early))
    matrices = [in_vmem(m) for m in matrices]
    coefficients = jnp.pad(column, (0, planes - STEPS))
    coefficients = jnp.broadcast_to(coefficients[None, :, None], (1, planes, width))
    halves = pl.pallas_call(
        functools.partial(halves_kernel, cells),
        out_shape=pltpu.VMEM((len(arrived) * (cells // 2) + 1, planes, width), f32),
        in_specs=[vmem] * (1 + len(arrived)),
        out_specs=vmem,
    )(*[in_vmem(x) for x in [coefficients] + arrived])
    swapped = lax.ppermute(halves, "orb", xor_pairs(n_orb, 1))

    operands = matrices + [in_vmem(x) for x in [packed] + arrived]
    start, taps = pl.pallas_call(
        functools.partial(open_kernel, layout),
        out_shape=(padded, window),
        in_specs=[vmem] * len(operands),
        out_specs=(vmem, vmem),
    )(*operands)
    operands = matrices + [in_vmem(x) for x in [potential, swapped, start, taps] + arrived]
    panel = pl.pallas_call(
        functools.partial(chain_kernel, layout),
        out_shape=slab,
        in_specs=[smem] + [vmem] * len(operands),
        out_specs=vmem,
        scratch_shapes=[padded, padded, window],
    )(pltpu.with_memory_space_constraint(degree, pltpu.SMEM), *operands)

    *near, last = sorted(range(2, n_orb, 2), key=lambda m: (m % 4 == 2, m))
    far = lax.ppermute(jnp.broadcast_to(column[:, None], (STEPS, width)), "orb", xor_pairs(n_orb, last))

    def weights(columns, held):
        chosen = (owners[:, None] == jnp.stack([me ^ m for m in held])[None, :]).astype(f32)
        return jnp.sum(jnp.stack(columns)[:, :, None, :] * chosen[None, :, :, None], 1)

    def combined(columns, held, panels):
        return pl.pallas_call(
            functools.partial(combine_kernel, len(panels)),
            out_shape=(slab,) * len(columns),
            in_specs=[vmem] * (1 + len(panels)),
            out_specs=(vmem,) * len(columns),
        )(in_vmem(weights(columns, held)), *[in_vmem(p) for p in panels])

    panels = [panel] + [lax.ppermute(panel, "orb", xor_pairs(n_orb, m)) for m in near]
    beside = lax.ppermute(panel, "orb", xor_pairs(n_orb, 1))
    (sent,) = combined([far], [0, 1], [panel, beside])
    received = lax.ppermute(sent, "orb", xor_pairs(n_orb, last))
    mine, theirs = combined([coefficients[0, :STEPS], swapped[-1, :STEPS]], [0] + near, panels)
    rotated = mine + lax.ppermute(theirs, "orb", xor_pairs(n_orb, 1)) + received
    return tuple(jnp.transpose(x, (1, 0, 2))[None] for x in (panel, rotated))


def solution(mesh):
    placed = (
        P("orb", None, "dom", None),
        P(None, "dom", None),
        P("orb"),
        P(),
        P(None, None, "orb"),
    )
    return jax.shard_map(
        per_device,
        mesh=mesh,
        in_specs=placed,
        out_specs=(P("orb", None, "dom", None), P("orb", None, "dom", None)),
        check_vma=False,
    )
```
